128 devices in a mesh: scene: 2 (over core), row: 8 (over x, y_lo), col: 8 (over z, y_hi).
Axes of the slice: x: 4, y: 4 (y_hi: 2, y_lo: 2; y = y_hi * 2 + y_lo), z: 4, core: 2. Of those that a mesh axis runs over, the one named last changes fastest.
Arguments:
- activations: bfloat16 [384, 256, 768], P(('scene', 'row'), 'col'), parts along dimension 0, may hold values from -6 to 6
- cotangent: bfloat16 [384, 256, 768], P(('scene', 'row'), 'col'), parts along dimension 0, may hold values from -6 to 6
- qkv_weight: bfloat16 [768, 2304], replicated, may hold values from -1 to 1
- out_weight: bfloat16 [768, 768], replicated, may hold values from -0.21875 to 0.21875
Outputs:
- input_grad: bfloat16 [384, 256, 768], P(('scene', 'row'), 'col'), parts along dimension 0
- qkv_weight_grad: float32 [1536, 2304], P(('scene', 'row', 'col')), parts along dimension 0
- out_weight_grad: float32 [1536, 768], P(('scene', 'row', 'col')), parts along dimension 0
The draws below stay inside these ranges and needn't reach their ends.
There are 2 independent parts, one for each index of `scene`. The reference program is written for one: setup_inputs(seed, part) draws one part's arguments, and reference() takes and returns one part's arrays. A program takes and returns all parts, laid end to end along the dimension named above; an argument that names none is the same for every part. Nothing has to cross between parts.
All inputs are finite; a program needn't handle non-finite values.
Results may differ from the reference program's by a relative error of at most 0.0096.
Values may be sent and summed in bfloat16 or wider, within the bound.
No kernel may reach another device: no remote copies, remote signals or barrier semaphores. Data moves between devices by JAX's collectives and lax.ppermute only.
A program may use at most 128 MiB of HBM per device.

```python
import jax
import jax.numpy as jnp
from jax import lax

D = 768
HEADS = 24
ROWS_DEV = 24
COLS_DEV = 32
ROWS = 192
COLS = 256
N_ROW = 8
N_COL = 8


def draw_qkv_weight(key, part):
    key = jax.random.fold_in(key, 11)
    first_key = jax.random.fold_in(key, 0)
    head_dim = D // HEADS
    spread = D ** (-0.5)
    full = jnp.clip(jax.random.normal(first_key, (D, 3, HEADS, head_dim), jnp.float32), -6.0, 6.0) * spread
    return full.reshape(D, 3 * D).astype(jnp.bfloat16)


def raised(values, stream_key, source, target, blocks, factor):
    def block_of(axis_at):
        return (jnp.arange(values.shape[axis_at]) // (values.shape[axis_at] // blocks)).reshape((-1,) + (1,) * (values.ndim - 1 - axis_at))

    near = jax.random.permutation(stream_key, blocks)[block_of(target)]
    second = (block_of(target) + blocks // 2) % blocks
    return jnp.where((block_of(source) == near) | (block_of(source) == second), factor * values, values)


def shard_levels(own_key, dims, cuts, low, top_value):
    gain = 1.0
    for dim, blocks in cuts:
        heights = jax.random.uniform(jax.random.fold_in(jax.random.fold_in(own_key, 6), dim), (blocks,), jnp.float32, low / len(cuts), top_value / len(cuts))
        gain = gain * jnp.repeat(jnp.exp(heights), dims[dim] // blocks).reshape((-1,) + (1,) * (len(dims) - 1 - dim))
    return gain


def bell_draw(key, extent, scale, reach, shards=(), kind=jnp.bfloat16):
    level = shard_levels(key, extent, shards, -0.22, 0.18) if shards else 1.0
    array = jax.random.normal(key, extent, jnp.float32) * scale * level
    return jnp.minimum(jnp.maximum(array, -reach), reach).astype(kind)


def gaussian_with(key, dims, width, limit, pieces, heavy, kind=jnp.bfloat16):
    values = width * jax.random.normal(key, dims, jnp.float32)
    if pieces:
        values = values * shard_levels(key, dims, pieces, -0.22, 0.18)
    return jnp.clip(raised(values, jax.random.fold_in(key, 3), *heavy), -limit, limit).astype(kind)


def setup_inputs(seed: int = 0, part: int = 0) -> dict:
    keys = jax.random.split(jax.random.key(seed), 5)
    own_keys = jax.random.split(jax.random.fold_in(keys[4], part), 5)
    return {
        "activations": gaussian_with(own_keys[0], (ROWS, COLS, D), 1.0, 6.0, ((0, 8), (1, 8)), (0, 2, 8, 2.0)),
        "cotangent": bell_draw(own_keys[1], (ROWS, COLS, D), 1.0, 6.0, ((0, 8), (1, 8))),
        "qkv_weight": draw_qkv_weight(jax.random.fold_in(keys[4], 71), part),
        "out_weight": bell_draw(keys[3], (D, D), D ** -0.5, 0.21875),
    }


EPSILON = 1e-05

def layer_normalize(tokens):
    value_rows = tokens.astype(jnp.float32)
    centred = value_rows - lax.optimization_barrier(jnp.mean(value_rows, axis=-1, keepdims=True))
    inverse_deviation = lax.rsqrt(lax.optimization_barrier(jnp.mean(centred * centred, axis=-1, keepdims=True)) + EPSILON)
    return (centred * inverse_deviation, inverse_deviation)

def group_backward(activation_windows, cot_groups, qkv_weight, out_weight):
    element_count, sequence_length, feature_width = activation_windows.shape
    head_dim = feature_width // HEADS
    scaling = head_dim ** (-0.5)
    standardized_input, inverse_deviation = layer_normalize(activation_windows)
    normalized_input = standardized_input.astype(jnp.bfloat16).reshape(element_count * sequence_length, feature_width)
    projected = jnp.dot(normalized_input, qkv_weight, preferred_element_type=jnp.float32).astype(jnp.bfloat16)
    projected = projected.reshape(element_count, sequence_length, 3, HEADS, head_dim).astype(jnp.float32)
    query_rows, key_rows, value_rows = (projected[:, :, 0], projected[:, :, 1], projected[:, :, 2])
    scores = jnp.einsum('nqhd,nkhd->nhqk', query_rows, key_rows) * scaling
    attention_weights = jax.nn.softmax(scores, axis=-1)
    weights_reduced = attention_weights.astype(jnp.bfloat16).astype(jnp.float32)
    attention_output = jnp.einsum('nhqk,nkhd->nqhd', weights_reduced, value_rows)
    attention_output = attention_output.astype(jnp.bfloat16).reshape(element_count * sequence_length, feature_width)
    cot_rows = cot_groups.reshape(element_count * sequence_length, feature_width)
    out_grad = jnp.dot(cot_rows, out_weight.T, preferred_element_type=jnp.float32).astype(jnp.bfloat16)
    out_grad = out_grad.reshape(element_count, sequence_length, HEADS, head_dim).astype(jnp.float32)
    out_term = jnp.dot(attention_output.T, cot_rows, preferred_element_type=jnp.float32)
    prob_grad = jnp.einsum('nqhd,nkhd->nhqk', out_grad, value_rows)
    value_grad = jnp.einsum('nhqk,nqhd->nkhd', weights_reduced, out_grad)
    score_grad = attention_weights * (prob_grad - lax.optimization_barrier(jnp.sum(attention_weights * prob_grad, axis=-1, keepdims=True)))
    score_low = score_grad.astype(jnp.bfloat16).astype(jnp.float32)
    query_grad = jnp.einsum('nhqk,nkhd->nqhd', score_low, key_rows) * scaling
    key_grad = jnp.einsum('nhqk,nqhd->nkhd', score_low, query_rows) * scaling
    qkv_grad = jnp.stack([query_grad, key_grad, value_grad], axis=2).astype(jnp.bfloat16)
    qkv_grad = qkv_grad.reshape(element_count * sequence_length, 3 * feature_width)
    qkv_term = jnp.dot(normalized_input.T, qkv_grad, preferred_element_type=jnp.float32)
    normalized_gradient = jnp.dot(qkv_grad, qkv_weight.T, preferred_element_type=jnp.float32)
    normalized_gradient = normalized_gradient.reshape(element_count, sequence_length, feature_width)
    centered_gradient = normalized_gradient - lax.optimization_barrier(jnp.mean(normalized_gradient, axis=-1, keepdims=True))
    centered_gradient = centered_gradient - standardized_input * lax.optimization_barrier(jnp.mean(normalized_gradient * standardized_input, axis=-1, keepdims=True))
    input_grad = (cot_groups.astype(jnp.float32) + inverse_deviation * centered_gradient).astype(jnp.bfloat16)
    return (input_grad, qkv_term, out_term)

def to_groups(field):
    shaped = field.reshape(N_ROW, ROWS_DEV, N_COL, COLS_DEV, D)
    return shaped.transpose(1, 3, 0, 2, 4).reshape(ROWS_DEV, COLS_DEV, N_ROW * N_COL, D)

def reference(activations, cotangent, qkv_weight, out_weight):
    activation_windows = to_groups(activations)
    cot_groups = to_groups(cotangent)

    def one_row(carry, pair):
        grad_groups, qkv_term, out_term = group_backward(pair[0], pair[1], qkv_weight, out_weight)
        return ((carry[0] + qkv_term, carry[1] + out_term), grad_groups)
    start_sums = (jnp.zeros((D, 3 * D), jnp.float32), jnp.zeros((D, D), jnp.float32))
    (qkv_weight_grad, out_weight_grad), grad_groups = lax.scan(one_row, start_sums, (activation_windows, cot_groups))
    input_grad = grad_groups.reshape(ROWS_DEV, COLS_DEV, N_ROW, N_COL, D).transpose(2, 0, 3, 1, 4)
    input_grad = input_grad.reshape(ROWS, COLS, D)
    return (input_grad, qkv_weight_grad, out_weight_grad)
```

```python
import functools

import jax
import jax.numpy as jnp
from jax import lax
from jax.experimental import pallas as pl
from jax.experimental.pallas import tpu as pltpu
from jax.sharding import PartitionSpec as P

HEADS = 24
EPSILON = 1e-05
BF16 = jnp.bfloat16
F32 = jnp.float32
MIB = 1 << 20


def dot(a, b, dims):
    return lax.dot_general(a, b, ((dims[0], dims[1]), ((), ())), preferred_element_type=F32)


def nn(a, b):
    return dot(a, b, ((1,), (0,)))


def nt(a, b):
    return dot(a, b, ((1,), (1,)))


def tn(a, b):
    return dot(a, b, ((0,), (0,)))


def one_hot(shape, column_of_row):
    rows = lax.broadcasted_iota(jnp.int32, shape, 0)
    columns = lax.broadcasted_iota(jnp.int32, shape, 1)
    return jnp.where(columns == column_of_row(rows), 1.0, 0.0).astype(BF16)


def pack_kernel(act_main, act_tail, cot_main, cot_tail, out):
    rows, width = act_main.shape
    half = width // 2
    upper = one_hot((rows, rows // 2), lambda i: jnp.where(i % 8 < 4, (i // 8) * 4 + i % 4, -1))
    lower = one_hot((rows, rows // 2), lambda i: jnp.where(i % 8 < 4, -1, (i // 8) * 4 + i % 4))
    at = 0
    for main, tail in ((act_main, act_tail), (cot_main, cot_tail)):
        out[:, at : at + width] = main[...]
        packed = nn(upper, tail[:, :half]) + nn(lower, tail[:, half:])
        out[:, at + width : at + width + half] = packed.astype(BF16)
        at += width + half


def pack_tokens(act, cot, peers):
    tokens, width = act.shape
    steps = 4
    rows = peers * 8 // steps
    main = pl.BlockSpec((rows, width), lambda i: (i, 0))
    tail = pl.BlockSpec((rows // 2, width), lambda i: (2 * steps + i, 0))
    return pl.pallas_call(
        pack_kernel,
        grid=(steps,),
        in_specs=[main, tail, main, tail],
        out_specs=pl.BlockSpec((rows, 3 * width), lambda i: (i, 0)),
        out_shape=jax.ShapeDtypeStruct((peers * 8, 3 * width), BF16),
        compiler_params=pltpu.CompilerParams(vmem_limit_bytes=32 * MIB),
        name="pack_tokens",
    )(act, act, cot, cot)


def main_kernel(
    got, qkv_w, out_w, out, xs, ns, cs, qkv, og, dqkv, att, ngs, mean_s, inv_s, nt1, nt2, at1, at2, order
):
    width = out_w.shape[0]
    half = width // 2
    tokens = xs.shape[0]
    seq = 64
    main = got.shape[0]
    rest = tokens - main
    packed = width + half
    head_dim = width // HEADS
    scaling = head_dim**-0.5

    order[...] = one_hot((main, main), lambda k: (k % seq) * 8 + k // seq)
    for first, to in ((0, xs), (packed, cs)):
        for c in range(0, width, half):
            to[:main, c : c + half] = nn(order[...], got[:, first + c : first + c + half]).astype(BF16)
        tail = nn(order[...], got[:, first + width : first + packed]).astype(BF16)
        to[main:, :half] = tail[:rest]
        to[main:, half:] = tail[rest:]

    @pl.loop(0, tokens // seq)
    def _(g):
        rows = pl.ds(pl.multiple_of(g * seq, seq), seq)
        x = xs[rows, :].astype(F32)
        mean = jnp.mean(x, axis=-1, keepdims=True)
        centred = x - mean
        inv = lax.rsqrt(jnp.mean(centred * centred, axis=-1, keepdims=True) + EPSILON)
        ns[rows, :] = (centred * inv).astype(BF16)
        mean_s[rows, :] = jnp.broadcast_to(mean, (seq, 128))
        inv_s[rows, :] = jnp.broadcast_to(inv, (seq, 128))

    @pl.loop(0, 3 * width // 256)
    def _(j):
        cols = pl.ds(pl.multiple_of(j * 256, 256), 256)
        qkv[:, cols] = nn(ns[...], qkv_w[:, cols]).astype(BF16)

    @pl.loop(0, width // 256)
    def _(j):
        cols = pl.ds(pl.multiple_of(j * 256, 256), 256)
        og[:, cols] = nt(cs[...], out_w[cols, :]).astype(BF16)

    lanes = 128
    heads = lanes // head_dim
    wide = heads * seq
    own = lax.broadcasted_iota(jnp.int32, (wide, lanes), 0) // seq
    keep = jnp.where(lax.broadcasted_iota(jnp.int32, (wide, lanes), 1) // head_dim == own, 1.0, 0.0).astype(BF16)
    lane_head = lax.broadcasted_iota(jnp.int32, (seq, lanes), 1) // head_dim

    def spread(x):
        return jnp.concatenate([x] * heads, axis=0) * keep

    def fold(x):
        total = x[:seq]
        for h in range(1, heads):
            total = jnp.where(lane_head == h, x[h * seq : (h + 1) * seq], total)
        return total

    @pl.loop(0, tokens // seq)
    def _(g):
        rows = pl.ds(pl.multiple_of(g * seq, seq), seq)
        for c in range(0, width, lanes):
            q = qkv[rows, c : c + lanes]
            k = qkv[rows, width + c : width + c + lanes]
            v = qkv[rows, 2 * width + c : 2 * width + c + lanes]
            q_wide = spread(q)
            g_wide = spread(og[rows, c : c + lanes])
            scores = nt(k, q_wide)
            top = jnp.max(scores, axis=0, keepdims=True)
            e = jnp.exp((scores - top) * scaling)
            probs = e * (1.0 / jnp.sum(e, axis=0, keepdims=True))
            probs_low = probs.astype(BF16)
            prob_grad = nt(v, g_wide)
            delta = jnp.sum(probs * prob_grad, axis=0, keepdims=True)
            score_low = (probs * (prob_grad - delta)).astype(BF16)
            att[rows, c : c + lanes] = fold(tn(probs_low, v)).astype(BF16)
            dqkv[rows, c : c + lanes] = (fold(tn(score_low, k)) * scaling).astype(BF16)
            dqkv[rows, width + c : width + c + lanes] = (nn(score_low, q_wide) * scaling).astype(BF16)
            dqkv[rows, 2 * width + c : 2 * width + c + lanes] = nn(probs_low, g_wide).astype(BF16)

    @pl.loop(0, width // 256)
    def _(j):
        cols = pl.ds(pl.multiple_of(j * 256, 256), 256)
        ngs[:, cols] = nt(dqkv[...], qkv_w[cols, :])

    @pl.loop(0, tokens // seq)
    def _(g):
        rows = pl.ds(pl.multiple_of(g * seq, seq), seq)
        inv = inv_s[rows, :][:, :1]
        xhat = (xs[rows, :].astype(F32) - mean_s[rows, :][:, :1]) * inv
        ng = ngs[rows, :]
        centred = ng - jnp.mean(ng, axis=-1, keepdims=True)
        centred = centred - xhat * jnp.mean(ng * xhat, axis=-1, keepdims=True)
        xs[rows, :] = (cs[rows, :].astype(F32) + inv * centred).astype(BF16)

    back = one_hot((main, main), lambda i: (i % 8) * seq + i // 8)
    for c in range(0, width, half):
        out[:, c : c + half] = nn(back, xs[:main, c : c + half]).astype(BF16)
    tail = nn(back[:, :rest], xs[main:, :half]) + nn(back[:, rest:], xs[main:, half:])
    out[:, width:packed] = tail.astype(BF16)

    eight = one_hot((main, width), lambda i: (i // 8) * 12 + i % 8)
    four = one_hot((main, width), lambda i: (i // 8) * 12 + 8 + i % 4)
    nt1[...] = nt(eight, ns[...]).astype(BF16)
    nt2[...] = nt(four, ns[...]).astype(BF16)
    at1[...] = nt(eight, att[...]).astype(BF16)
    at2[...] = nt(four, att[...]).astype(BF16)

    @pl.loop(0, 3 * width // 256)
    def _(j):
        cols = pl.ds(pl.multiple_of(j * 256, 256), 256)
        to = pl.ds(pl.multiple_of(packed + j * 256, 128), 256)
        out[:, to] = nn(nt1[...], dqkv[:, cols]).astype(BF16)

    @pl.loop(0, width // 256)
    def _(j):
        cols = pl.ds(pl.multiple_of(j * 256, 256), 256)
        to = pl.ds(pl.multiple_of(packed + 3 * width + j * 256, 128), 256)
        out[:, to] = nn(at1[...], cs[:, cols]).astype(BF16)

    first = packed + 4 * width
    is_upper = lax.broadcasted_iota(jnp.int32, (main, 256), 0) % 8 < 4

    @pl.loop(0, width // 256)
    def _(j):
        a = pl.ds(pl.multiple_of(j * 256, 256), 256)
        b = pl.ds(pl.multiple_of(2 * width + j * 256, 256), 256)
        to = pl.ds(pl.multiple_of(first + j * 256, 128), 256)
        pair = jnp.where(is_upper, nn(nt2[...], dqkv[:, a]), nn(nt2[...], dqkv[:, b]))
        out[:, to] = pair.astype(BF16)

    @pl.loop(0, width // 256)
    def _(j):
        a = pl.ds(pl.multiple_of(width + j * 256, 256), 256)
        b = pl.ds(pl.multiple_of(j * 256, 256), 256)
        to = pl.ds(pl.multiple_of(first + width + j * 256, 128), 256)
        pair = jnp.where(is_upper, nn(nt2[...], dqkv[:, a]), nn(at2[...], cs[:, b]))
        out[:, to] = pair.astype(BF16)


def group_backward(got, qkv_weight, out_weight, tokens):
    width = out_weight.shape[0]
    main = got.shape[0]
    vmem = pl.BlockSpec(memory_space=pltpu.VMEM)
    square = (tokens, width)
    scratch = [
        pltpu.VMEM(square, BF16),
        pltpu.VMEM(square, BF16),
        pltpu.VMEM(square, BF16),
        pltpu.VMEM((tokens, 3 * width), BF16),
        pltpu.VMEM(square, BF16),
        pltpu.VMEM((tokens, 3 * width), BF16),
        pltpu.VMEM(square, BF16),
        pltpu.VMEM(square, F32),
        pltpu.VMEM((tokens, 128), F32),
        pltpu.VMEM((tokens, 128), F32),
        pltpu.VMEM((main, tokens), BF16),
        pltpu.VMEM((main, tokens), BF16),
        pltpu.VMEM((main, tokens), BF16),
        pltpu.VMEM((main, tokens), BF16),
        pltpu.VMEM((main, main), BF16),
    ]
    return pl.pallas_call(
        main_kernel,
        in_specs=[vmem] * 3,
        out_specs=vmem,
        out_shape=jax.ShapeDtypeStruct((main, 3 * width // 2 + 6 * width), BF16),
        scratch_shapes=scratch,
        compiler_params=pltpu.CompilerParams(vmem_limit_bytes=56 * MIB),
        name="group_backward",
    )(got, qkv_weight, out_weight)


def finish_kernel(got, grad, qkv_grad, out_grad, total):
    step = pl.program_id(0)
    rows = got.shape[0]
    width = grad.shape[1]
    half = width // 2
    packed = width + half
    main = 8 * grad.shape[0] // 12
    grad[pl.ds(pl.multiple_of(step * rows, 16), rows), :] = got[:, :width]
    pick = one_hot((rows // 2, rows), lambda k: (k // 4) * 8 + k % 4)
    pick_low = one_hot((rows // 2, rows), lambda k: (k // 4) * 8 + 4 + k % 4)
    tail = pl.ds(pl.multiple_of(main + step * (rows // 2), 16), rows // 2)
    grad[tail, :half] = nn(pick, got[:, width:packed]).astype(BF16)
    grad[tail, half:] = nn(pick_low, got[:, width:packed]).astype(BF16)

    @pl.when(step == 0)
    def _():
        total[...] = jnp.zeros_like(total)

    cols = 4 * width + 2 * width
    for c in range(0, cols, width):
        part = got[:, packed + c : packed + c + width].astype(F32).reshape(rows // 8, 8, width)
        total[:, c : c + width] += jnp.sum(part, axis=0)

    @pl.when(step == pl.num_programs(0) - 1)
    def _():
        qkv_grad[:8, :] = total[:, : 3 * width]
        out_grad[:8, :] = total[:, 3 * width : 4 * width]
        qkv_grad[8:12, : 2 * width] = total[:4, 4 * width :]
        qkv_grad[8:12, 2 * width :] = total[4:, 4 * width : 5 * width]
        out_grad[8:12, :] = total[4:, 5 * width :]


def finish(got, tokens, width):
    steps = 4
    rows = got.shape[0] // steps
    whole = lambda shape: pl.BlockSpec(shape, lambda i: (0, 0))
    shapes = ((tokens, width), (12, 3 * width), (12, width))
    return pl.pallas_call(
        finish_kernel,
        grid=(steps,),
        in_specs=[pl.BlockSpec((rows, got.shape[1]), lambda i: (i, 0))],
        out_specs=[whole(s) for s in shapes],
        out_shape=[jax.ShapeDtypeStruct(s, d) for s, d in zip(shapes, (BF16, F32, F32), strict=True)],
        scratch_shapes=[pltpu.VMEM((8, 6 * width), F32)],
        compiler_params=pltpu.CompilerParams(vmem_limit_bytes=32 * MIB),
        name="finish",
    )(got)


def local(activations, cotangent, qkv_weight, out_weight):
    peers = lax.axis_size("row") * lax.axis_size("col")
    rows_dev, cols_dev, width = activations.shape
    tokens = rows_dev * cols_dev
    exchange = functools.partial(
        lax.all_to_all, axis_name=("row", "col"), split_axis=0, concat_axis=0, tiled=True
    )
    sent = pack_tokens(activations.reshape(tokens, width), cotangent.reshape(tokens, width), peers)
    grads = group_backward(exchange(sent), qkv_weight, out_weight, tokens)
    input_grad, qkv_weight_grad, out_weight_grad = finish(exchange(grads), tokens, width)
    return (input_grad.reshape(rows_dev, cols_dev, width), qkv_weight_grad, out_weight_grad)


def solution(mesh):
    return jax.shard_map(
        local,
        mesh=mesh,
        in_specs=(P(("scene", "row"), "col", None), P(("scene", "row"), "col", None), P(), P()),
        out_specs=(
            P(("scene", "row"), "col", None),
            P(("scene", "row", "col"), None),
            P(("scene", "row", "col"), None),
        ),
        check_vma=False,
    )
```

```python
import functools

import jax
import jax.numpy as jnp
from jax import lax
from jax.experimental import pallas as pl
from jax.experimental.pallas import tpu as pltpu
from jax.sharding import PartitionSpec as P

HEADS = 24
EPSILON = 1e-05
BF16 = jnp.bfloat16
F32 = jnp.float32
MIB = 1 << 20


def dot(a, b, dims):
    return lax.dot_general(a, b, ((dims[0], dims[1]), ((), ())), preferred_element_type=F32)


def nn(a, b):
    return dot(a, b, ((1,), (0,)))


def nt(a, b):
    return dot(a, b, ((1,), (1,)))


def tn(a, b):
    return dot(a, b, ((0,), (0,)))


def one_hot(shape, column_of_row):
    rows = lax.broadcasted_iota(jnp.int32, shape, 0)
    columns = lax.broadcasted_iota(jnp.int32, shape, 1)
    return jnp.where(columns == column_of_row(rows), 1.0, 0.0).astype(BF16)


def pack_kernel(act_main, act_tail, cot_main, cot_tail, out):
    rows, width = act_main.shape
    half = width // 2
    upper = one_hot((rows, rows // 2), lambda i: jnp.where(i % 8 < 4, (i // 8) * 4 + i % 4, -1))
    lower = one_hot((rows, rows // 2), lambda i: jnp.where(i % 8 < 4, -1, (i // 8) * 4 + i % 4))
    at = 0
    for main, tail in ((act_main, act_tail), (cot_main, cot_tail)):
        out[:, at : at + width] = main[...]
        packed = nn(upper, tail[:, :half]) + nn(lower, tail[:, half:])
        out[:, at + width : at + width + half] = packed.astype(BF16)
        at += width + half


def pack_tokens(act, cot, peers):
    tokens, width = act.shape
    steps = 4
    rows = peers * 8 // steps
    main = pl.BlockSpec((rows, width), lambda i: (i, 0))
    tail = pl.BlockSpec((rows // 2, width), lambda i: (2 * steps + i, 0))
    return pl.pallas_call(
        pack_kernel,
        grid=(steps,),
        in_specs=[main, tail, main, tail],
        out_specs=pl.BlockSpec((rows, 3 * width), lambda i: (i, 0)),
        out_shape=jax.ShapeDtypeStruct((peers * 8, 3 * width), BF16),
        compiler_params=pltpu.CompilerParams(vmem_limit_bytes=32 * MIB),
        name="pack_tokens",
    )(act, act, cot, cot)


def main_kernel(
    got, qkv_w, out_w, out, xs, ns, cs, qkv, og, dqkv, att, ngs, mean_s, inv_s, nt1, nt2, at1, at2, order
):
    width = out_w.shape[0]
    half = width // 2
    tokens = xs.shape[0]
    seq = 64
    main = got.shape[0]
    rest = tokens - main
    packed = width + half
    head_dim = width // HEADS
    scaling = head_dim**-0.5

    order[...] = one_hot((main, main), lambda k: (k % seq) * 8 + k // seq)
    for first, to in ((0, xs), (packed, cs)):
        for c in range(0, width, half):
            to[:main, c : c + half] = nn(order[...], got[:, first + c : first + c + half]).astype(BF16)
        tail = nn(order[...], got[:, first + width : first + packed]).astype(BF16)
        to[main:, :half] = tail[:rest]
        to[main:, half:] = tail[rest:]

    @pl.loop(0, tokens // seq, unroll=4)
    def _(g):
        rows = pl.ds(pl.multiple_of(g * seq, seq), seq)
        x = xs[rows, :].astype(F32)
        mean = jnp.mean(x, axis=-1, keepdims=True)
        centred = x - mean
        inv = lax.rsqrt(jnp.mean(centred * centred, axis=-1, keepdims=True) + EPSILON)
        ns[rows, :] = (centred * inv).astype(BF16)
        mean_s[rows, :] = jnp.broadcast_to(mean, (seq, 128))
        inv_s[rows, :] = jnp.broadcast_to(inv, (seq, 128))

    @pl.loop(0, 3 * width // 256, unroll=3)
    def _(j):
        cols = pl.ds(pl.multiple_of(j * 256, 256), 256)
        qkv[:, cols] = nn(ns[...], qkv_w[:, cols]).astype(BF16)

    @pl.loop(0, width // 256, unroll=3)
    def _(j):
        cols = pl.ds(pl.multiple_of(j * 256, 256), 256)
        og[:, cols] = nt(cs[...], out_w[cols, :]).astype(BF16)

    lanes = 128
    heads = lanes // head_dim
    wide = heads * seq
    own = lax.broadcasted_iota(jnp.int32, (wide, lanes), 0) // seq
    keep = jnp.where(lax.broadcasted_iota(jnp.int32, (wide, lanes), 1) // head_dim == own, 1.0, 0.0).astype(BF16)
    lane_head = lax.broadcasted_iota(jnp.int32, (seq, lanes), 1) // head_dim

    def spread(x):
        return jnp.concatenate([x] * heads, axis=0) * keep

    def fold(x):
        total = x[:seq]
        for h in range(1, heads):
            total = jnp.where(lane_head == h, x[h * seq : (h + 1) * seq], total)
        return total

    @pl.loop(0, tokens // seq, unroll=2)
    def _(g):
        rows = pl.ds(pl.multiple_of(g * seq, seq), seq)
        blocks = range(0, width, lanes)
        queries = [qkv[rows, c : c + lanes] for c in blocks]
        keys = [qkv[rows, width + c : width + c + lanes] for c in blocks]
        values = [qkv[rows, 2 * width + c : 2 * width + c + lanes] for c in blocks]
        q_wide = [spread(q) for q in queries]
        g_wide = [spread(og[rows, c : c + lanes]) for c in blocks]
        scores = [nt(k, q) for k, q in zip(keys, q_wide)]
        prob_grads = [nt(v, g) for v, g in zip(values, g_wide)]
        probs_low, score_low = [], []
        for score, prob_grad in zip(scores, prob_grads):
            top = jnp.max(score, axis=0, keepdims=True)
            e = jnp.exp((score - top) * scaling)
            probs = e * (1.0 / jnp.sum(e, axis=0, keepdims=True))
            delta = jnp.sum(probs * prob_grad, axis=0, keepdims=True)
            probs_low.append(probs.astype(BF16))
            score_low.append((probs * (prob_grad - delta)).astype(BF16))
        value_grads = [nn(p, g) for p, g in zip(probs_low, g_wide)]
        key_grads = [nn(s, q) for s, q in zip(score_low, q_wide)]
        attended = [tn(p, v) for p, v in zip(probs_low, values)]
        query_grads = [tn(s, k) for s, k in zip(score_low, keys)]
        for i, c in enumerate(blocks):
            dqkv[rows, width + c : width + c + lanes] = (key_grads[i] * scaling).astype(BF16)
            dqkv[rows, 2 * width + c : 2 * width + c + lanes] = value_grads[i].astype(BF16)
            att[rows, c : c + lanes] = fold(attended[i]).astype(BF16)
            dqkv[rows, c : c + lanes] = (fold(query_grads[i]) * scaling).astype(BF16)

    @pl.loop(0, width // 256, unroll=3)
    def _(j):
        cols = pl.ds(pl.multiple_of(j * 256, 256), 256)
        ngs[:, cols] = nt(dqkv[...], qkv_w[cols, :])

    @pl.loop(0, tokens // seq, unroll=4)
    def _(g):
        rows = pl.ds(pl.multiple_of(g * seq, seq), seq)
        inv = inv_s[rows, :][:, :1]
        xhat = (xs[rows, :].astype(F32) - mean_s[rows, :][:, :1]) * inv
        ng = ngs[rows, :]
        centred = ng - jnp.mean(ng, axis=-1, keepdims=True)
        centred = centred - xhat * jnp.mean(ng * xhat, axis=-1, keepdims=True)
        xs[rows, :] = (cs[rows, :].astype(F32) + inv * centred).astype(BF16)

    back = one_hot((main, main), lambda i: (i % 8) * seq + i // 8)
    for c in range(0, width, half):
        out[:, c : c + half] = nn(back, xs[:main, c : c + half]).astype(BF16)
    tail = nn(back[:, :rest], xs[main:, :half]) + nn(back[:, rest:], xs[main:, half:])
    out[:, width:packed] = tail.astype(BF16)

    eight = one_hot((main, width), lambda i: (i // 8) * 12 + i % 8)
    four = one_hot((main, width), lambda i: (i // 8) * 12 + 8 + i % 4)
    nt1[...] = nt(eight, ns[...]).astype(BF16)
    nt2[...] = nt(four, ns[...]).astype(BF16)
    at1[...] = nt(eight, att[...]).astype(BF16)
    at2[...] = nt(four, att[...]).astype(BF16)

    @pl.loop(0, 3 * width // 256, unroll=3)
    def _(j):
        cols = pl.ds(pl.multiple_of(j * 256, 256), 256)
        to = pl.ds(pl.multiple_of(packed + j * 256, 128), 256)
        out[:, to] = nn(nt1[...], dqkv[:, cols]).astype(BF16)

    @pl.loop(0, width // 256, unroll=3)
    def _(j):
        cols = pl.ds(pl.multiple_of(j * 256, 256), 256)
        to = pl.ds(pl.multiple_of(packed + 3 * width + j * 256, 128), 256)
        out[:, to] = nn(at1[...], cs[:, cols]).astype(BF16)

    first = packed + 4 * width
    is_upper = lax.broadcasted_iota(jnp.int32, (main, 256), 0) % 8 < 4

    @pl.loop(0, width // 256, unroll=3)
    def _(j):
        a = pl.ds(pl.multiple_of(j * 256, 256), 256)
        b = pl.ds(pl.multiple_of(2 * width + j * 256, 256), 256)
        to = pl.ds(pl.multiple_of(first + j * 256, 128), 256)
        pair = jnp.where(is_upper, nn(nt2[...], dqkv[:, a]), nn(nt2[...], dqkv[:, b]))
        out[:, to] = pair.astype(BF16)

    @pl.loop(0, width // 256, unroll=3)
    def _(j):
        a = pl.ds(pl.multiple_of(width + j * 256, 256), 256)
        b = pl.ds(pl.multiple_of(j * 256, 256), 256)
        to = pl.ds(pl.multiple_of(first + width + j * 256, 128), 256)
        pair = jnp.where(is_upper, nn(nt2[...], dqkv[:, a]), nn(at2[...], cs[:, b]))
        out[:, to] = pair.astype(BF16)


def group_backward(got, qkv_weight, out_weight, tokens):
    width = out_weight.shape[0]
    main = got.shape[0]
    vmem = pl.BlockSpec(memory_space=pltpu.VMEM)
    square = (tokens, width)
    scratch = [
        pltpu.VMEM(square, BF16),
        pltpu.VMEM(square, BF16),
        pltpu.VMEM(square, BF16),
        pltpu.VMEM((tokens, 3 * width), BF16),
        pltpu.VMEM(square, BF16),
        pltpu.VMEM((tokens, 3 * width), BF16),
        pltpu.VMEM(square, BF16),
        pltpu.VMEM(square, F32),
        pltpu.VMEM((tokens, 128), F32),
        pltpu.VMEM((tokens, 128), F32),
        pltpu.VMEM((main, tokens), BF16),
        pltpu.VMEM((main, tokens), BF16),
        pltpu.VMEM((main, tokens), BF16),
        pltpu.VMEM((main, tokens), BF16),
        pltpu.VMEM((main, main), BF16),
    ]
    return pl.pallas_call(
        main_kernel,
        in_specs=[vmem] * 3,
        out_specs=vmem,
        out_shape=jax.ShapeDtypeStruct((main, 3 * width // 2 + 6 * width), BF16),
        scratch_shapes=scratch,
        compiler_params=pltpu.CompilerParams(vmem_limit_bytes=38 * MIB),
        name="group_backward",
    )(got, qkv_weight, out_weight)


def finish_kernel(got, grad, qkv_grad, out_grad, total):
    step = pl.program_id(0)
    rows = got.shape[0]
    width = grad.shape[1]
    half = width // 2
    packed = width + half
    main = 8 * grad.shape[0] // 12
    grad[pl.ds(pl.multiple_of(step * rows, 16), rows), :] = got[:, :width]
    pick = one_hot((rows // 2, rows), lambda k: (k // 4) * 8 + k % 4)
    pick_low = one_hot((rows // 2, rows), lambda k: (k // 4) * 8 + 4 + k % 4)
    tail = pl.ds(pl.multiple_of(main + step * (rows // 2), 16), rows // 2)
    grad[tail, :half] = nn(pick, got[:, width:packed]).astype(BF16)
    grad[tail, half:] = nn(pick_low, got[:, width:packed]).astype(BF16)

    @pl.when(step == 0)
    def _():
        total[...] = jnp.zeros_like(total)

    cols = 4 * width + 2 * width
    for c in range(0, cols, width):
        part = got[:, packed + c : packed + c + width].astype(F32).reshape(rows // 8, 8, width)
        total[:, c : c + width] += jnp.sum(part, axis=0)

    @pl.when(step == pl.num_programs(0) - 1)
    def _():
        qkv_grad[:8, :] = total[:, : 3 * width]
        out_grad[:8, :] = total[:, 3 * width : 4 * width]
        qkv_grad[8:12, : 2 * width] = total[:4, 4 * width :]
        qkv_grad[8:12, 2 * width :] = total[4:, 4 * width : 5 * width]
        out_grad[8:12, :] = total[4:, 5 * width :]


def finish(got, tokens, width):
    steps = 4
    rows = got.shape[0] // steps
    whole = lambda shape: pl.BlockSpec(shape, lambda i: (0, 0))
    shapes = ((tokens, width), (12, 3 * width), (12, width))
    return pl.pallas_call(
        finish_kernel,
        grid=(steps,),
        in_specs=[pl.BlockSpec((rows, got.shape[1]), lambda i: (i, 0))],
        out_specs=[whole(s) for s in shapes],
        out_shape=[jax.ShapeDtypeStruct(s, d) for s, d in zip(shapes, (BF16, F32, F32), strict=True)],
        scratch_shapes=[pltpu.VMEM((8, 6 * width), F32)],
        compiler_params=pltpu.CompilerParams(vmem_limit_bytes=32 * MIB),
        name="finish",
    )(got)


def local(activations, cotangent, qkv_weight, out_weight):
    peers = lax.axis_size("row") * lax.axis_size("col")
    rows_dev, cols_dev, width = activations.shape
    tokens = rows_dev * cols_dev
    exchange = functools.partial(
        lax.all_to_all, axis_name=("row", "col"), split_axis=0, concat_axis=0, tiled=True
    )
    sent = pack_tokens(activations.reshape(tokens, width), cotangent.reshape(tokens, width), peers)
    grads = group_backward(exchange(sent), qkv_weight, out_weight, tokens)
    input_grad, qkv_weight_grad, out_weight_grad = finish(exchange(grads), tokens, width)
    return (input_grad.reshape(rows_dev, cols_dev, width), qkv_weight_grad, out_weight_grad)


def solution(mesh):
    return jax.shard_map(
        local,
        mesh=mesh,
        in_specs=(P(("scene", "row"), "col", None), P(("scene", "row"), "col", None), P(), P()),
        out_specs=(
            P(("scene", "row"), "col", None),
            P(("scene", "row", "col"), None),
            P(("scene", "row", "col"), None),
        ),
        check_vma=False,
    )
```

```python
import functools

import jax
import jax.numpy as jnp
from jax import lax
from jax.experimental import pallas as pl
from jax.experimental.pallas import tpu as pltpu
from jax.sharding import PartitionSpec as P

HEADS = 24
EPSILON = 1e-05
BF16 = jnp.bfloat16
F32 = jnp.float32
MIB = 1 << 20


SEQ = 64
LANES = 128
PAIRS = (("row", 2, 4, 2), ("row", 6, 5, 2), ("row", 1, 3, 2), ("col", 2, 1, 2), ("col", 6, 2, 1))
TILE = 256


def dot(a, b, dims):
    return lax.dot_general(a, b, ((dims[0], dims[1]), ((), ())), preferred_element_type=F32)


def nn(a, b):
    return dot(a, b, ((1,), (0,)))


def nt(a, b):
    return dot(a, b, ((1,), (1,)))


def tn(a, b):
    return dot(a, b, ((0,), (0,)))


def one_hot(shape, column_of_row):
    rows = lax.broadcasted_iota(jnp.int32, shape, 0)
    columns = lax.broadcasted_iota(jnp.int32, shape, 1)
    return jnp.where(columns == column_of_row(rows), 1.0, 0.0).astype(BF16)


def pack_kernel(act_main, act_tail, cot_main, cot_tail, out):
    rows, width = act_main.shape
    half = width // 2
    upper = one_hot((rows, rows // 2), lambda i: jnp.where(i % 8 < 4, (i // 8) * 4 + i % 4, -1))
    lower = one_hot((rows, rows // 2), lambda i: jnp.where(i % 8 < 4, -1, (i // 8) * 4 + i % 4))
    at = 0
    for main, tail in ((act_main, act_tail), (cot_main, cot_tail)):
        out[:, at : at + width] = main[...]
        packed = nn(upper, tail[:, :half]) + nn(lower, tail[:, half:])
        out[:, at + width : at + width + half] = packed.astype(BF16)
        at += width + half


def pack_tokens(act, cot, peers):
    tokens, width = act.shape
    steps = 4
    rows = peers * 8 // steps
    main = pl.BlockSpec((rows, width), lambda i: (i, 0))
    tail = pl.BlockSpec((rows // 2, width), lambda i: (2 * steps + i, 0))
    return pl.pallas_call(
        pack_kernel,
        grid=(steps,),
        in_specs=[main, tail, main, tail],
        out_specs=pl.BlockSpec((rows, 3 * width), lambda i: (i, 0)),
        out_shape=jax.ShapeDtypeStruct((peers * 8, 3 * width), BF16),
        compiler_params=pltpu.CompilerParams(vmem_limit_bytes=32 * MIB),
        name="pack_tokens",
    )(act, act, cot, cot)


def parameters(limit, flops=0, moved=0):
    return dict(
        compiler_params=pltpu.CompilerParams(vmem_limit_bytes=limit * MIB),
        cost_estimate=pl.CostEstimate(flops=flops, bytes_accessed=moved, transcendentals=0),
    )


def rows_of(g):
    return pl.ds(pl.multiple_of(g * SEQ, SEQ), SEQ)


def project(ns, cs, qkv_w, out_w, qkv, og):
    for c in range(0, qkv.shape[1], 256):
        qkv[:, c : c + 256] = nn(ns[...], qkv_w[:, c : c + 256]).astype(BF16)
    for c in range(0, og.shape[1], 256):
        og[:, c : c + 256] = nt(cs[...], out_w[c : c + 256, :]).astype(BF16)


def attend(qkv, og, dqkv, att, together):
    tokens, count = og.shape
    head_dim = 32
    scaling = head_dim**-0.5
    heads = LANES // head_dim
    shape = (heads * SEQ, LANES)
    own = lax.broadcasted_iota(jnp.int32, shape, 0) // SEQ
    keep = jnp.where(lax.broadcasted_iota(jnp.int32, shape, 1) // head_dim == own, 1.0, 0.0).astype(BF16)
    lane_head = lax.broadcasted_iota(jnp.int32, (SEQ, LANES), 1) // head_dim

    def spread(x):
        return jnp.concatenate([x] * heads, axis=0) * keep

    def fold(x):
        total = x[:SEQ]
        for h in range(1, heads):
            total = jnp.where(lane_head == h, x[h * SEQ : (h + 1) * SEQ], total)
        return total

    @pl.loop(0, tokens // SEQ // together)
    def _(step):
        blocks = [(rows_of(step * together + g), c) for g in range(together) for c in range(0, count, LANES)]
        queries = [qkv[rows, c : c + LANES] for rows, c in blocks]
        keys = [qkv[rows, count + c : count + c + LANES] for rows, c in blocks]
        values = [qkv[rows, 2 * count + c : 2 * count + c + LANES] for rows, c in blocks]
        q_wide = [spread(q) for q in queries]
        g_wide = [spread(og[rows, c : c + LANES]) for rows, c in blocks]
        scores = [nt(k, q) for k, q in zip(keys, q_wide)]
        prob_grads = [nt(v, g) for v, g in zip(values, g_wide)]
        probs_low, score_low = [], []
        for score, prob_grad in zip(scores, prob_grads):
            top = jnp.max(score, axis=0, keepdims=True)
            e = jnp.exp((score - top) * scaling)
            probs = e * (1.0 / jnp.sum(e, axis=0, keepdims=True))
            delta = jnp.sum(probs * prob_grad, axis=0, keepdims=True)
            probs_low.append(probs.astype(BF16))
            score_low.append((probs * (prob_grad - delta)).astype(BF16))
        value_grads = [nn(p, g) for p, g in zip(probs_low, g_wide)]
        key_grads = [nn(s, q) for s, q in zip(score_low, q_wide)]
        attended = [tn(p, v) for p, v in zip(probs_low, values)]
        query_grads = [tn(s, k) for s, k in zip(score_low, keys)]
        for i, (rows, c) in enumerate(blocks):
            dqkv[rows, count + c : count + c + LANES] = (key_grads[i] * scaling).astype(BF16)
            dqkv[rows, 2 * count + c : 2 * count + c + LANES] = value_grads[i].astype(BF16)
            att[rows, c : c + LANES] = fold(attended[i]).astype(BF16)
            dqkv[rows, c : c + LANES] = (fold(query_grads[i]) * scaling).astype(BF16)


def eight_rows(shape):
    return one_hot(shape, lambda i: (i // 8) * 12 + i % 8)


def four_rows(shape):
    return one_hot(shape, lambda i: (i // 8) * 12 + 8 + i % 4)


def main_kernel(
    bits, got, qkv_w, out_w, xs, cs, stats, dqkv, *refs
):
    kept, sent = refs[: len(PAIRS)], refs[len(PAIRS) : 2 * len(PAIRS)]
    ns, nt1, nt2, at1, at2, att, qkv, og, order = refs[2 * len(PAIRS) :]
    width = out_w.shape[0]
    half = width // 2
    tokens = xs.shape[0]
    main = got.shape[0]
    rest = tokens - main
    packed = width + half

    order[...] = one_hot((main, main), lambda k: (k % SEQ) * 8 + k // SEQ)
    for first, to in ((0, xs), (packed, cs)):
        for c in range(0, width, half):
            to[:main, c : c + half] = nn(order[...], got[:, first + c : first + c + half]).astype(BF16)
        tail = nn(order[...], got[:, first + width : first + packed]).astype(BF16)
        to[main:, :half] = tail[:rest]
        to[main:, half:] = tail[rest:]

    @pl.loop(0, tokens // SEQ, unroll=4)
    def _(g):
        rows = rows_of(g)
        x = xs[rows, :].astype(F32)
        mean = jnp.mean(x, axis=-1, keepdims=True)
        centred = x - mean
        inv = lax.rsqrt(jnp.mean(centred * centred, axis=-1, keepdims=True) + EPSILON)
        ns[rows, :] = (centred * inv).astype(BF16)
        stats[rows, :LANES] = jnp.broadcast_to(mean, (SEQ, LANES))
        stats[rows, LANES:] = jnp.broadcast_to(inv, (SEQ, LANES))

    project(ns, cs, qkv_w, out_w, qkv, og)
    attend(qkv, og, dqkv, att, 2)

    eight, four = eight_rows((main, width)), four_rows((main, width))
    for pick, source, to in ((eight, ns, nt1), (four, ns, nt2), (eight, att, at1), (four, att, at2)):
        to[...] = nt(pick, source[...]).astype(BF16)
    tile = TILE
    shape = (main, tile)
    place = lax.broadcasted_iota(jnp.int32, shape, 0)
    is_upper = place % 8 < 4

    def share(keep, send, c, low, high, direction):
        same = (place // (8 << PAIRS[direction][2])) % 2 == bits[direction]
        keep[:, c : c + tile] = jnp.where(same, low, high).astype(BF16)
        send[:, c : c + tile] = jnp.where(same, high, low).astype(BF16)

    places = [(i, c) for i, pair in enumerate(PAIRS) for c in range(0, pair[3] * tile, tile)]
    for c in range(0, width, tile):
        q, k, v = (slice(part * width + c, part * width + c + tile) for part in range(3))
        for kind in range(3):
            if kind == 0:
                low, high = nn(nt1[...], dqkv[:, q]), nn(nt1[...], dqkv[:, k])
            elif kind == 1:
                low, high = nn(nt1[...], dqkv[:, v]), nn(at1[...], cs[:, q])
            else:
                low = jnp.where(is_upper, nn(nt2[...], dqkv[:, q]), nn(nt2[...], dqkv[:, v]))
                high = jnp.where(is_upper, nn(nt2[...], dqkv[:, k]), nn(at2[...], cs[:, q]))
            direction, to = places[kind * (width // tile) + c // tile]
            share(kept[direction], sent[direction], to, low, high, direction)


def main_part(bits, got, qkv_weight, out_weight, tokens):
    width = out_weight.shape[0]
    main = got.shape[0]
    vmem = pl.BlockSpec(memory_space=pltpu.VMEM)
    square = (tokens, width)
    outs = [(square, BF16), (square, BF16), ((tokens, 2 * LANES), F32), ((tokens, 3 * width), BF16)]
    outs += [((main, pair[3] * TILE), BF16) for pair in PAIRS * 2]
    return pl.pallas_call(
        main_kernel,
        in_specs=[pl.BlockSpec(memory_space=pltpu.SMEM)] + [vmem] * 3,
        out_specs=[vmem] * len(outs),
        out_shape=[jax.ShapeDtypeStruct(s, d) for s, d in outs],
        scratch_shapes=[pltpu.VMEM(square, BF16)]
        + [pltpu.VMEM((main, tokens), BF16)] * 4
        + [
            pltpu.VMEM(square, BF16),
            pltpu.VMEM((tokens, 3 * width), BF16),
            pltpu.VMEM(square, BF16),
            pltpu.VMEM((main, main), BF16),
        ],
        name="main_part",
        **parameters(34, 16 * 10**9, 30 * 10**6),
    )(bits, got, qkv_weight, out_weight)


def token_kernel(xs, cs, stats, dqkv, qkv_w, out, ngs, igs):
    tokens, width = xs.shape
    main = out.shape[0]
    rest = tokens - main
    half = width // 2
    for f in range(0, width, 256):
        ngs[:, f : f + 256] = nt(dqkv[...], qkv_w[f : f + 256, :])

    @pl.loop(0, tokens // SEQ, unroll=4)
    def _(g):
        rows = rows_of(g)
        inv = stats[rows, LANES:][:, :1]
        xhat = (xs[rows, :].astype(F32) - stats[rows, :LANES][:, :1]) * inv
        ng = ngs[rows, :]
        centred = ng - jnp.mean(ng, axis=-1, keepdims=True)
        centred = centred - xhat * jnp.mean(ng * xhat, axis=-1, keepdims=True)
        igs[rows, :] = (cs[rows, :].astype(F32) + inv * centred).astype(BF16)

    back = one_hot((main, main), lambda i: (i % 8) * SEQ + i // 8)
    for c in range(0, width, half):
        out[:, c : c + half] = nn(back, igs[:main, c : c + half]).astype(BF16)
    tail = nn(back[:, :rest], igs[main:, :half]) + nn(back[:, rest:], igs[main:, half:])
    out[:, width:] = tail.astype(BF16)


def token_part(xs, cs, stats, dqkv, qkv_weight, main):
    tokens, width = xs.shape
    vmem = pl.BlockSpec(memory_space=pltpu.VMEM)
    return pl.pallas_call(
        token_kernel,
        in_specs=[vmem] * 5,
        out_specs=vmem,
        out_shape=jax.ShapeDtypeStruct((main, width + width // 2), BF16),
        scratch_shapes=[pltpu.VMEM((tokens, width), F32), pltpu.VMEM((tokens, width), BF16)],
        name="token_grad",
        **parameters(20, 4 * 10**9, 12 * 10**6),
    )(xs, cs, stats, dqkv, qkv_weight)


def join_kernel(grad, *refs):
    *pairs, out = refs
    at = grad.shape[1]
    out[:, :at] = grad[...]
    for keep, came in zip(pairs[: len(PAIRS)], pairs[len(PAIRS) :], strict=True):
        count = keep.shape[1]
        out[:, at : at + count] = (keep[...].astype(F32) + came[...].astype(F32)).astype(BF16)
        at += count


def join(grad, pairs):
    rows = grad.shape[0]
    arrays = [grad, *pairs]
    width = grad.shape[1] + sum(a.shape[1] for a in pairs) // 2
    block = lambda count: pl.BlockSpec((rows // 4, count), lambda i: (i, 0))
    return pl.pallas_call(
        join_kernel,
        grid=(4,),
        in_specs=[block(a.shape[1]) for a in arrays],
        out_specs=block(width),
        out_shape=jax.ShapeDtypeStruct((rows, width), BF16),
        name="join",
        **parameters(16, 0, 8 * 10**6),
    )(*arrays)


def finish_kernel(bits, got, grad, qkv_grad, out_grad, total):
    step = pl.program_id(0)
    rows = got.shape[0]
    width = grad.shape[1]
    half = width // 2
    packed = width + half
    main = 8 * grad.shape[0] // 12
    grad[pl.ds(pl.multiple_of(step * rows, 16), rows), :] = got[:, :width]
    pick = one_hot((rows // 2, rows), lambda k: (k // 4) * 8 + k % 4)
    pick_low = one_hot((rows // 2, rows), lambda k: (k // 4) * 8 + 4 + k % 4)
    tail = pl.ds(pl.multiple_of(main + step * (rows // 2), 16), rows // 2)
    grad[tail, :half] = nn(pick, got[:, width:packed]).astype(BF16)
    grad[tail, half:] = nn(pick_low, got[:, width:packed]).astype(BF16)

    @pl.when(step == 0)
    def _():
        total[...] = jnp.zeros_like(total)

    blocks = width // TILE
    places = [i for i, pair in enumerate(PAIRS) for _ in range(pair[3])]
    for block, direction in enumerate(places):
        first = packed + block * TILE
        came = got[:, first : first + TILE].astype(F32)
        bit = PAIRS[direction][2]
        if rows <= 8 << bit:
            every = came.reshape(-1, 8, TILE).sum(axis=0)
            odd = (step * rows // (8 << bit)) % 2 == 1
            low, high = jnp.where(odd, 0.0, every), jnp.where(odd, every, 0.0)
        else:
            runs = came.reshape(-1, 8 << bit, TILE)
            low = sum(runs[i].reshape(-1, 8, TILE).sum(axis=0) for i in range(0, runs.shape[0], 2))
            high = sum(runs[i].reshape(-1, 8, TILE).sum(axis=0) for i in range(1, runs.shape[0], 2))
        at = (2 * (block // blocks) * blocks + block % blocks) * TILE
        total[:, at : at + TILE] += jnp.where(bits[direction] == 0, low, high)
        total[:, at + width : at + width + TILE] += jnp.where(bits[direction] == 0, high, low)

    @pl.when(step == pl.num_programs(0) - 1)
    def _():
        q, k, v, o, low, high = (total[:, i * width : (i + 1) * width] for i in range(6))
        for part, (top, end) in enumerate(((q, low[:4]), (k, high[:4]), (v, low[4:]))):
            qkv_grad[:8, part * width : (part + 1) * width] = top
            qkv_grad[8:12, part * width : (part + 1) * width] = end
        out_grad[:8, :] = o
        out_grad[8:12, :] = high[4:]


def finish(bits, got, tokens, width):
    steps = 4
    rows = got.shape[0] // steps
    whole = lambda shape: pl.BlockSpec(shape, lambda i: (0, 0))
    shapes = ((tokens, width), (12, 3 * width), (12, width))
    return pl.pallas_call(
        finish_kernel,
        grid=(steps,),
        in_specs=[pl.BlockSpec(memory_space=pltpu.SMEM), pl.BlockSpec((rows, got.shape[1]), lambda i: (i, 0))],
        out_specs=[whole(s) for s in shapes],
        out_shape=[jax.ShapeDtypeStruct(s, d) for s, d in zip(shapes, (BF16, F32, F32), strict=True)],
        scratch_shapes=[pltpu.VMEM((8, 6 * width), F32)],
        name="finish",
        **parameters(24, 10**9, 5 * 10**6),
    )(bits, got)


def local(activations, cotangent, qkv_weight, out_weight):
    grid_rows, grid_cols = lax.axis_size("row"), lax.axis_size("col")
    peers = grid_rows * grid_cols
    rows_dev, cols_dev, width = activations.shape
    tokens = rows_dev * cols_dev
    exchange = functools.partial(
        lax.all_to_all, axis_name=("row", "col"), split_axis=0, concat_axis=0, tiled=True
    )
    row, col = lax.axis_index("row"), lax.axis_index("col")
    place = row * grid_cols + col
    bits = jnp.stack([place // (1 << bit) % 2 for _, _, bit, _ in PAIRS]).astype(jnp.int32)
    sent = pack_tokens(activations.reshape(tokens, width), cotangent.reshape(tokens, width), peers)
    sent, bits = lax.optimization_barrier((sent, bits))
    xs, cs, stats, dqkv, *pairs = main_part(bits, exchange(sent), qkv_weight, out_weight, tokens)
    came = [
        lax.ppermute(x, axis, [(i, i ^ other) for i in range(lax.axis_size(axis))])
        for x, (axis, other, _, _) in zip(pairs[len(PAIRS) :], PAIRS, strict=True)
    ]
    grads = token_part(xs, cs, stats, dqkv, qkv_weight, peers * 8)
    got = exchange(join(grads, (*pairs[: len(PAIRS)], *came)))
    input_grad, qkv_weight_grad, out_weight_grad = finish(bits, got, tokens, width)
    return (input_grad.reshape(rows_dev, cols_dev, width), qkv_weight_grad, out_weight_grad)


def solution(mesh):
    return jax.shard_map(
        local,
        mesh=mesh,
        in_specs=(P(("scene", "row"), "col", None), P(("scene", "row"), "col", None), P(), P()),
        out_specs=(
            P(("scene", "row"), "col", None),
            P(("scene", "row", "col"), None),
            P(("scene", "row", "col"), None),
        ),
        check_vma=False,
    )
```

```python
import functools

import jax
import jax.numpy as jnp
from jax import lax
from jax.experimental import pallas as pl
from jax.experimental.pallas import tpu as pltpu
from jax.sharding import PartitionSpec as P

HEADS = 24
EPSILON = 1e-05
BF16 = jnp.bfloat16
F32 = jnp.float32
MIB = 1 << 20


SEQ = 64
LANES = 128
STREAMS = (
    ((16, 4), (8, 3), 2),
    ((48, 5), (2, 1), 2),
    ((8, 3), (16, 4), 2),
    ((2, 1), (48, 5), 2),
    ((6, 2), (9, 0), 1),
)
TILE = 256


def dot(a, b, dims):
    return lax.dot_general(a, b, ((dims[0], dims[1]), ((), ())), preferred_element_type=F32)


def nn(a, b):
    return dot(a, b, ((1,), (0,)))


def nt(a, b):
    return dot(a, b, ((1,), (1,)))


def tn(a, b):
    return dot(a, b, ((0,), (0,)))


def one_hot(shape, column_of_row):
    rows = lax.broadcasted_iota(jnp.int32, shape, 0)
    columns = lax.broadcasted_iota(jnp.int32, shape, 1)
    return jnp.where(columns == column_of_row(rows), 1.0, 0.0).astype(BF16)


def pack_kernel(act_main, act_tail, cot_main, cot_tail, out):
    rows, width = act_main.shape
    half = width // 2
    upper = one_hot((rows, rows // 2), lambda i: jnp.where(i % 8 < 4, (i // 8) * 4 + i % 4, -1))
    lower = one_hot((rows, rows // 2), lambda i: jnp.where(i % 8 < 4, -1, (i // 8) * 4 + i % 4))
    at = 0
    for main, tail in ((act_main, act_tail), (cot_main, cot_tail)):
        out[:, at : at + width] = main[...]
        packed = nn(upper, tail[:, :half]) + nn(lower, tail[:, half:])
        out[:, at + width : at + width + half] = packed.astype(BF16)
        at += width + half


def pack_tokens(act, cot, peers):
    tokens, width = act.shape
    steps = 4
    rows = peers * 8 // steps
    main = pl.BlockSpec((rows, width), lambda i: (i, 0))
    tail = pl.BlockSpec((rows // 2, width), lambda i: (2 * steps + i, 0))
    return pl.pallas_call(
        pack_kernel,
        grid=(steps,),
        in_specs=[main, tail, main, tail],
        out_specs=pl.BlockSpec((rows, 3 * width), lambda i: (i, 0)),
        out_shape=jax.ShapeDtypeStruct((peers * 8, 3 * width), BF16),
        compiler_params=pltpu.CompilerParams(vmem_limit_bytes=32 * MIB),
        name="pack_tokens",
    )(act, act, cot, cot)


def parameters(limit, flops=0, moved=0):
    return dict(
        compiler_params=pltpu.CompilerParams(vmem_limit_bytes=limit * MIB),
        cost_estimate=pl.CostEstimate(flops=flops, bytes_accessed=moved, transcendentals=0),
    )


def is_own(row, bits, bit):
    return (row // (8 << bit)) % 2 == bits[bit]


def rows_of(g):
    return pl.ds(pl.multiple_of(g * SEQ, SEQ), SEQ)


def project(ns, cs, qkv_w, out_w, qkv, og):
    for c in range(0, qkv.shape[1], 256):
        qkv[:, c : c + 256] = nn(ns[...], qkv_w[:, c : c + 256]).astype(BF16)
    for c in range(0, og.shape[1], 256):
        og[:, c : c + 256] = nt(cs[...], out_w[c : c + 256, :]).astype(BF16)


def attend(qkv, og, dqkv, att, together):
    tokens, count = og.shape
    head_dim = 32
    scaling = head_dim**-0.5
    heads = LANES // head_dim
    shape = (heads * SEQ, LANES)
    own = lax.broadcasted_iota(jnp.int32, shape, 0) // SEQ
    keep = jnp.where(lax.broadcasted_iota(jnp.int32, shape, 1) // head_dim == own, 1.0, 0.0).astype(BF16)
    lane_head = lax.broadcasted_iota(jnp.int32, (SEQ, LANES), 1) // head_dim

    def spread(x):
        return jnp.concatenate([x] * heads, axis=0) * keep

    def fold(x):
        total = x[:SEQ]
        for h in range(1, heads):
            total = jnp.where(lane_head == h, x[h * SEQ : (h + 1) * SEQ], total)
        return total

    @pl.loop(0, tokens // SEQ // together)
    def _(step):
        blocks = [(rows_of(step * together + g), c) for g in range(together) for c in range(0, count, LANES)]
        queries = [qkv[rows, c : c + LANES] for rows, c in blocks]
        keys = [qkv[rows, count + c : count + c + LANES] for rows, c in blocks]
        values = [qkv[rows, 2 * count + c : 2 * count + c + LANES] for rows, c in blocks]
        q_wide = [spread(q) for q in queries]
        g_wide = [spread(og[rows, c : c + LANES]) for rows, c in blocks]
        scores = [nt(k, q) for k, q in zip(keys, q_wide)]
        prob_grads = [nt(v, g) for v, g in zip(values, g_wide)]
        probs_low, score_low = [], []
        for score, prob_grad in zip(scores, prob_grads):
            top = jnp.max(score, axis=0, keepdims=True)
            e = jnp.exp((score - top) * scaling)
            probs = e * (1.0 / jnp.sum(e, axis=0, keepdims=True))
            delta = jnp.sum(probs * prob_grad, axis=0, keepdims=True)
            probs_low.append(probs.astype(BF16))
            score_low.append((probs * (prob_grad - delta)).astype(BF16))
        value_grads = [nn(p, g) for p, g in zip(probs_low, g_wide)]
        key_grads = [nn(s, q) for s, q in zip(score_low, q_wide)]
        attended = [tn(p, v) for p, v in zip(probs_low, values)]
        query_grads = [tn(s, k) for s, k in zip(score_low, keys)]
        for i, (rows, c) in enumerate(blocks):
            dqkv[rows, count + c : count + c + LANES] = (key_grads[i] * scaling).astype(BF16)
            dqkv[rows, 2 * count + c : 2 * count + c + LANES] = value_grads[i].astype(BF16)
            att[rows, c : c + LANES] = fold(attended[i]).astype(BF16)
            dqkv[rows, c : c + LANES] = (fold(query_grads[i]) * scaling).astype(BF16)


def eight_rows(shape):
    return one_hot(shape, lambda i: (i // 8) * 12 + i % 8)


def four_rows(shape):
    return one_hot(shape, lambda i: (i // 4) * 12 + 8 + i % 4)


def main_kernel(
    bits, got, qkv_w, out_w, xs, cs, stats, dqkv, *refs
):
    count = len(STREAMS)
    kept, sent = refs[:count], refs[count : 2 * count]
    ns, nt1, nt2, at1, at2, att, qkv, og, order = refs[2 * count :]
    width = out_w.shape[0]
    half = width // 2
    tokens = xs.shape[0]
    main = got.shape[0]
    rest = tokens - main
    packed = width + half

    order[...] = one_hot((main, main), lambda k: (k % SEQ) * 8 + k // SEQ)
    for first, to in ((0, xs), (packed, cs)):
        for c in range(0, width, half):
            to[:main, c : c + half] = nn(order[...], got[:, first + c : first + c + half]).astype(BF16)
        tail = nn(order[...], got[:, first + width : first + packed]).astype(BF16)
        to[main:, :half] = tail[:rest]
        to[main:, half:] = tail[rest:]

    @pl.loop(0, tokens // SEQ, unroll=4)
    def _(g):
        rows = rows_of(g)
        x = xs[rows, :].astype(F32)
        mean = jnp.mean(x, axis=-1, keepdims=True)
        centred = x - mean
        inv = lax.rsqrt(jnp.mean(centred * centred, axis=-1, keepdims=True) + EPSILON)
        ns[rows, :] = (centred * inv).astype(BF16)
        stats[rows, :LANES] = jnp.broadcast_to(mean, (SEQ, LANES))
        stats[rows, LANES:] = jnp.broadcast_to(inv, (SEQ, LANES))

    project(ns, cs, qkv_w, out_w, qkv, og)
    attend(qkv, og, dqkv, att, 2)

    eight, four = eight_rows((main, width)), four_rows((main // 2, width))
    for pick, source, to in ((eight, ns, nt1), (four, ns, nt2), (eight, att, at1), (four, att, at2)):
        to[...] = nt(pick, source[...]).astype(BF16)
    tile = TILE
    shape = (main, tile)
    place = lax.broadcasted_iota(jnp.int32, shape, 0)
    is_upper = lax.broadcasted_iota(jnp.int32, (main // 16, 8, tile), 1) < 4

    def under(a, b):
        a, b = a.reshape(is_upper.shape), b.reshape(is_upper.shape)
        first = jnp.where(is_upper, a, pltpu.roll(b, 4, 1))
        second = jnp.where(is_upper, pltpu.roll(a, 4, 1), b)
        return jnp.stack([first, second], axis=1).reshape(shape)

    def share(keep, send, c, low, high, direction):
        same = is_own(place, bits, STREAMS[direction][0][1])
        keep[:, c : c + tile] = jnp.where(same, low, high).astype(BF16)
        send[:, c : c + tile] = jnp.where(same, high, low).astype(BF16)

    places = [(i, c) for i, pair in enumerate(STREAMS) for c in range(0, pair[2] * tile, tile)]
    for c in range(0, width, tile):
        q, k, v = (slice(part * width + c, part * width + c + tile) for part in range(3))
        for kind in range(3):
            if kind == 0:
                low, high = nn(nt1[...], dqkv[:, q]), nn(nt1[...], dqkv[:, k])
            elif kind == 1:
                low, high = nn(nt1[...], dqkv[:, v]), nn(at1[...], cs[:, q])
            else:
                low = under(nn(nt2[...], dqkv[:, q]), nn(nt2[...], dqkv[:, v]))
                high = under(nn(nt2[...], dqkv[:, k]), nn(at2[...], cs[:, q]))
            direction, to = places[kind * (width // tile) + c // tile]
            share(kept[direction], sent[direction], to, low, high, direction)


def main_part(bits, got, qkv_weight, out_weight, tokens):
    width = out_weight.shape[0]
    main = got.shape[0]
    vmem = pl.BlockSpec(memory_space=pltpu.VMEM)
    square = (tokens, width)
    outs = [(square, BF16), (square, BF16), ((tokens, 2 * LANES), F32), ((tokens, 3 * width), BF16)]
    outs += [((main, stream[2] * TILE), BF16) for stream in STREAMS * 2]
    return pl.pallas_call(
        main_kernel,
        in_specs=[pl.BlockSpec(memory_space=pltpu.SMEM)] + [vmem] * 3,
        out_specs=[vmem] * len(outs),
        out_shape=[jax.ShapeDtypeStruct(s, d) for s, d in outs],
        scratch_shapes=[pltpu.VMEM(square, BF16)]
        + [pltpu.VMEM((n, tokens), BF16) for n in (main, main // 2) * 2]
        + [
            pltpu.VMEM(square, BF16),
            pltpu.VMEM((tokens, 3 * width), BF16),
            pltpu.VMEM(square, BF16),
            pltpu.VMEM((main, main), BF16),
        ],
        name="main_part",
        **parameters(34, 16 * 10**9, 30 * 10**6),
    )(bits, got, qkv_weight, out_weight)


def token_kernel(xs, cs, stats, dqkv, qkv_w, out, ngs, igs):
    tokens, width = xs.shape
    main = out.shape[0]
    rest = tokens - main
    half = width // 2
    for f in range(0, width, 256):
        ngs[:, f : f + 256] = nt(dqkv[...], qkv_w[f : f + 256, :])

    @pl.loop(0, tokens // SEQ, unroll=4)
    def _(g):
        rows = rows_of(g)
        inv = stats[rows, LANES:][:, :1]
        xhat = (xs[rows, :].astype(F32) - stats[rows, :LANES][:, :1]) * inv
        ng = ngs[rows, :]
        centred = ng - jnp.mean(ng, axis=-1, keepdims=True)
        centred = centred - xhat * jnp.mean(ng * xhat, axis=-1, keepdims=True)
        igs[rows, :] = (cs[rows, :].astype(F32) + inv * centred).astype(BF16)

    back = one_hot((main, main), lambda i: (i % 8) * SEQ + i // 8)
    for c in range(0, width, half):
        out[:, c : c + half] = nn(back, igs[:main, c : c + half]).astype(BF16)
    tail = nn(back[:, :rest], igs[main:, :half]) + nn(back[:, rest:], igs[main:, half:])
    out[:, width:] = tail.astype(BF16)


def token_part(xs, cs, stats, dqkv, qkv_weight, main):
    tokens, width = xs.shape
    vmem = pl.BlockSpec(memory_space=pltpu.VMEM)
    return pl.pallas_call(
        token_kernel,
        in_specs=[vmem] * 5,
        out_specs=vmem,
        out_shape=jax.ShapeDtypeStruct((main, width + width // 2), BF16),
        scratch_shapes=[pltpu.VMEM((tokens, width), F32), pltpu.VMEM((tokens, width), BF16)],
        name="token_grad",
        **parameters(20, 4 * 10**9, 12 * 10**6),
    )(xs, cs, stats, dqkv, qkv_weight)


def join_kernel(bits, *refs):
    count = len(STREAMS)
    kept, came, kept_on, sent_on = (refs[i * count : (i + 1) * count] for i in range(4))
    half = TILE // 2
    for i, (_, (_, bit), blocks) in enumerate(STREAMS):
        for c in range(blocks):
            at = c * TILE
            both = kept[i][:, at : at + TILE].astype(F32) + came[i][:, at : at + TILE].astype(F32)
            low, high = both[:, :half], both[:, half:]
            same = is_own(lax.broadcasted_iota(jnp.int32, low.shape, 0), bits, bit)
            kept_on[i][:, c * half : (c + 1) * half] = jnp.where(same, low, high).astype(BF16)
            sent_on[i][:, c * half : (c + 1) * half] = jnp.where(same, high, low).astype(BF16)


def join(bits, pairs):
    vmem = pl.BlockSpec(memory_space=pltpu.VMEM)
    shapes = [(a.shape[0], a.shape[1] // 2) for a in pairs]
    return pl.pallas_call(
        join_kernel,
        in_specs=[pl.BlockSpec(memory_space=pltpu.SMEM)] + [vmem] * len(pairs),
        out_specs=[vmem] * len(pairs),
        out_shape=[jax.ShapeDtypeStruct(s, BF16) for s in shapes],
        name="join",
        **parameters(16, 0, 8 * 10**6),
    )(bits, *pairs)


def join_last_kernel(grad, *refs):
    *pairs, out = refs
    at = grad.shape[1]
    out[:, :at] = grad[...]
    for keep, came in zip(pairs[: len(STREAMS)], pairs[len(STREAMS) :], strict=True):
        count = keep.shape[1]
        out[:, at : at + count] = (keep[...].astype(F32) + came[...].astype(F32)).astype(BF16)
        at += count


def join_last(grad, pairs):
    vmem = pl.BlockSpec(memory_space=pltpu.VMEM)
    width = grad.shape[1] + sum(a.shape[1] for a in pairs) // 2
    return pl.pallas_call(
        join_last_kernel,
        in_specs=[vmem] * (1 + len(pairs)),
        out_specs=vmem,
        out_shape=jax.ShapeDtypeStruct((grad.shape[0], width), BF16),
        name="join_last",
        **parameters(16, 0, 4 * 10**6),
    )(grad, *pairs)


def finish_kernel(bits, got, grad, qkv_grad, out_grad, total):
    rows, width = got.shape[0], out_grad.shape[1]
    packed = width + width // 2
    grad[:rows, :] = got[:, :width]
    part = 128
    pick = one_hot((part // 2, part), lambda k: (k // 4) * 8 + k % 4)
    pick_low = one_hot((part // 2, part), lambda k: (k // 4) * 8 + 4 + k % 4)
    for i in range(0, rows, part):
        tail = slice(rows + i // 2, rows + (i + part) // 2)
        grad[tail, : width // 2] = nn(pick, got[i : i + part, width:packed]).astype(BF16)
        grad[tail, width // 2 :] = nn(pick_low, got[i : i + part, width:packed]).astype(BF16)
    peers = got.shape[0] // 8
    half = TILE // 2
    blocks = width // TILE
    places = [stream for stream in STREAMS for _ in range(stream[2])]
    for block, ((_, first), (_, second), _) in enumerate(places):
        at = packed + block * half
        came = got[:, at : at + half].astype(F32)
        sums = {}
        for s in range(peers):
            key = (s >> first) & 1, (s >> second) & 1
            more = came[8 * s : 8 * s + 8]
            sums[key] = sums[key] + more if key in sums else more
        at = (2 * (block // blocks) * blocks + block % blocks) * TILE
        for i in range(2):
            for j in range(2):
                mine = [jnp.where(bits[second] == j, sums[a, 0], sums[a, 1]) for a in range(2)]
                to = at + i * width + j * half
                total[:, to : to + half] = jnp.where(bits[first] == i, mine[0], mine[1])
    q, k, v, o, low, high = (total[:, i * width : (i + 1) * width] for i in range(6))
    for part, (top, end) in enumerate(((q, low[:4]), (k, high[:4]), (v, low[4:]))):
        qkv_grad[:8, part * width : (part + 1) * width] = top
        qkv_grad[8:12, part * width : (part + 1) * width] = end
    out_grad[:8, :] = o
    out_grad[8:12, :] = high[4:]


def finish(bits, got, tokens, width):
    vmem = pl.BlockSpec(memory_space=pltpu.VMEM)
    return pl.pallas_call(
        finish_kernel,
        in_specs=[pl.BlockSpec(memory_space=pltpu.SMEM), vmem],
        out_specs=[vmem] * 3,
        out_shape=[jax.ShapeDtypeStruct((tokens, width), BF16)]
        + [jax.ShapeDtypeStruct((12, n), F32) for n in (3 * width, width)],
        scratch_shapes=[pltpu.VMEM((8, 6 * width), F32)],
        name="finish",
        **parameters(16, 10**7, 2 * 10**6),
    )(bits, got)


def local(activations, cotangent, qkv_weight, out_weight):
    grid_rows, grid_cols = lax.axis_size("row"), lax.axis_size("col")
    peers = grid_rows * grid_cols
    rows_dev, cols_dev, width = activations.shape
    tokens = rows_dev * cols_dev
    exchange = functools.partial(
        lax.all_to_all, axis_name=("row", "col"), split_axis=0, concat_axis=0, tiled=True
    )
    row, col = lax.axis_index("row"), lax.axis_index("col")
    place = row * grid_cols + col
    bits = jnp.stack([place // (1 << bit) % 2 for bit in range(6)]).astype(jnp.int32)
    sent = pack_tokens(activations.reshape(tokens, width), cotangent.reshape(tokens, width), peers)
    sent, bits = lax.optimization_barrier((sent, bits))
    xs, cs, stats, dqkv, *pairs = main_part(bits, exchange(sent), qkv_weight, out_weight, tokens)
    count = len(STREAMS)

    def swap(arrays, level):
        return [
            lax.ppermute(x, ("row", "col"), [(i, i ^ stream[level][0]) for i in range(peers)])
            for x, stream in zip(arrays, STREAMS, strict=True)
        ]

    came = swap(pairs[count:], 0)
    grads = token_part(xs, cs, stats, dqkv, qkv_weight, peers * 8)
    grads, *came = lax.optimization_barrier((grads, *came))
    pairs = join(bits, (*pairs[:count], *came))
    got = exchange(join_last(grads, (*pairs[:count], *swap(pairs[count:], 1))))
    input_grad, qkv_weight_grad, out_weight_grad = finish(bits, got, tokens, width)
    return (input_grad.reshape(rows_dev, cols_dev, width), qkv_weight_grad, out_weight_grad)


def solution(mesh):
    return jax.shard_map(
        local,
        mesh=mesh,
        in_specs=(P(("scene", "row"), "col", None), P(("scene", "row"), "col", None), P(), P()),
        out_specs=(
            P(("scene", "row"), "col", None),
            P(("scene", "row", "col"), None),
            P(("scene", "row", "col"), None),
        ),
        check_vma=False,
    )
```

```python
import functools

import jax
import jax.numpy as jnp
from jax import lax
from jax.experimental import pallas as pl
from jax.experimental.pallas import tpu as pltpu
from jax.sharding import PartitionSpec as P

HEADS = 24
EPSILON = 1e-05
BF16 = jnp.bfloat16
F32 = jnp.float32
MIB = 1 << 20


SEQ = 64
LANES = 128
LOG2_E = 1.4426950408889634
FIRST = (((16, 4), (8, 3), 2), ((48, 5), (2, 1), 2), ((8, 3), (16, 4), 2))
LAST = (((2, 1), (48, 5), 2), ((6, 2), (9, 0), 1))
STREAMS = FIRST + LAST
TILE = 256


def dot(a, b, dims):
    return lax.dot_general(a, b, ((dims[0], dims[1]), ((), ())), preferred_element_type=F32)


def nn(a, b):
    return dot(a, b, ((1,), (0,)))


def nt(a, b):
    return dot(a, b, ((1,), (1,)))


def tn(a, b):
    return dot(a, b, ((0,), (0,)))


def one_hot(shape, column_of_row):
    rows = lax.broadcasted_iota(jnp.int32, shape, 0)
    columns = lax.broadcasted_iota(jnp.int32, shape, 1)
    return jnp.where(columns == column_of_row(rows), 1.0, 0.0).astype(BF16)


def pack_kernel(act_main, act_tail, cot_main, cot_tail, out):
    rows, width = act_main.shape
    half = width // 2
    upper = one_hot((rows, rows // 2), lambda i: jnp.where(i % 8 < 4, (i // 8) * 4 + i % 4, -1))
    lower = one_hot((rows, rows // 2), lambda i: jnp.where(i % 8 < 4, -1, (i // 8) * 4 + i % 4))
    at = 0
    for main, tail in ((act_main, act_tail), (cot_main, cot_tail)):
        out[:, at : at + width] = main[...]
        packed = nn(upper, tail[:, :half]) + nn(lower, tail[:, half:])
        out[:, at + width : at + width + half] = packed.astype(BF16)
        at += width + half


def pack_tokens(act, cot, peers):
    tokens, width = act.shape
    steps = 4
    rows = peers * 8 // steps
    main = pl.BlockSpec((rows, width), lambda i: (i, 0))
    tail = pl.BlockSpec((rows // 2, width), lambda i: (2 * steps + i, 0))
    return pl.pallas_call(
        pack_kernel,
        grid=(steps,),
        in_specs=[main, tail, main, tail],
        out_specs=pl.BlockSpec((rows, 3 * width), lambda i: (i, 0)),
        out_shape=jax.ShapeDtypeStruct((peers * 8, 3 * width), BF16),
        compiler_params=pltpu.CompilerParams(vmem_limit_bytes=32 * MIB),
        name="pack_tokens",
    )(act, act, cot, cot)


def parameters(limit, flops=0, moved=0):
    return dict(
        compiler_params=pltpu.CompilerParams(vmem_limit_bytes=limit * MIB),
        cost_estimate=pl.CostEstimate(flops=flops, bytes_accessed=moved, transcendentals=0),
    )


def is_own(row, bits, bit):
    return (row // (8 << bit)) % 2 == bits[bit]


def rows_of(g):
    return pl.ds(pl.multiple_of(g * SEQ, SEQ), SEQ)


def project(ns, cs, qkv_w, out_w, qkv, og):
    for c in range(0, qkv.shape[1], 256):
        qkv[:, c : c + 256] = nn(ns[...], qkv_w[:, c : c + 256]).astype(BF16)
    for c in range(0, og.shape[1], 256):
        og[:, c : c + 256] = nt(cs[...], out_w[c : c + 256, :]).astype(BF16)


def attend(qkv, og, dqkv, att, together):
    tokens, count = og.shape
    head_dim = 32
    scaling = head_dim**-0.5
    heads = LANES // head_dim
    shape = (heads * SEQ, LANES)
    own = lax.broadcasted_iota(jnp.int32, shape, 0) // SEQ
    keep = jnp.where(lax.broadcasted_iota(jnp.int32, shape, 1) // head_dim == own, 1.0, 0.0).astype(BF16)
    lane_head = lax.broadcasted_iota(jnp.int32, (SEQ, LANES), 1) // head_dim

    def spread(x):
        return jnp.concatenate([x] * heads, axis=0) * keep

    def fold(x):
        total = x[:SEQ]
        for h in range(1, heads):
            total = jnp.where(lane_head == h, x[h * SEQ : (h + 1) * SEQ], total)
        return total

    @pl.loop(0, tokens // SEQ // together)
    def _(step):
        blocks = [(rows_of(step * together + g), c) for g in range(together) for c in range(0, count, LANES)]
        queries = [qkv[rows, c : c + LANES] for rows, c in blocks]
        keys = [qkv[rows, count + c : count + c + LANES] for rows, c in blocks]
        values = [qkv[rows, 2 * count + c : 2 * count + c + LANES] for rows, c in blocks]
        q_wide = [spread(q) for q in queries]
        g_wide = [spread(og[rows, c : c + LANES]) for rows, c in blocks]
        scores = [nt(k, q) for k, q in zip(keys, q_wide)]
        prob_grads = [nt(v, g) for v, g in zip(values, g_wide)]
        probs_low, score_low = [], []
        for score, prob_grad in zip(scores, prob_grads):
            top = jnp.max(score, axis=0, keepdims=True)
            e = jnp.exp2((score - top) * (scaling * LOG2_E))
            probs = e * (1.0 / jnp.sum(e, axis=0, keepdims=True))
            delta = jnp.sum(probs * prob_grad, axis=0, keepdims=True)
            probs_low.append(probs.astype(BF16))
            score_low.append((probs * (prob_grad - delta)).astype(BF16))
        value_grads = [nn(p, g) for p, g in zip(probs_low, g_wide)]
        key_grads = [nn(s, q) for s, q in zip(score_low, q_wide)]
        attended = [tn(p, v) for p, v in zip(probs_low, values)]
        query_grads = [tn(s, k) for s, k in zip(score_low, keys)]
        for i, (rows, c) in enumerate(blocks):
            dqkv[rows, count + c : count + c + LANES] = (key_grads[i] * scaling).astype(BF16)
            dqkv[rows, 2 * count + c : 2 * count + c + LANES] = value_grads[i].astype(BF16)
            att[rows, c : c + LANES] = fold(attended[i]).astype(BF16)
            dqkv[rows, c : c + LANES] = (fold(query_grads[i]) * scaling).astype(BF16)


def eight_rows(shape):
    return one_hot(shape, lambda i: (i // 8) * 12 + i % 8)


def four_rows(shape):
    return one_hot(shape, lambda i: (i // 4) * 12 + 8 + i % 4)


def main_kernel(
    bits, got, qkv_w, out_w, xs, cs, stats, dqkv, *refs
):
    ns, att, *pairs = refs[: 2 + 2 * len(FIRST)]
    nt1, at1, qkv, og, order = refs[2 + 2 * len(FIRST) :]
    width = out_w.shape[0]
    half = width // 2
    tokens = xs.shape[0]
    main = got.shape[0]
    rest = tokens - main
    packed = width + half

    order[...] = one_hot((main, main), lambda k: (k % SEQ) * 8 + k // SEQ)
    for first, to in ((0, xs), (packed, cs)):
        for c in range(0, width, half):
            to[:main, c : c + half] = nn(order[...], got[:, first + c : first + c + half]).astype(BF16)
        tail = nn(order[...], got[:, first + width : first + packed]).astype(BF16)
        to[main:, :half] = tail[:rest]
        to[main:, half:] = tail[rest:]

    @pl.loop(0, tokens // SEQ, unroll=12)
    def _(g):
        rows = rows_of(g)
        x = xs[rows, :].astype(F32)
        mean = jnp.mean(x, axis=-1, keepdims=True)
        centred = x - mean
        inv = lax.rsqrt(jnp.mean(centred * centred, axis=-1, keepdims=True) + EPSILON)
        ns[rows, :] = (centred * inv).astype(BF16)
        stats[rows, :LANES] = jnp.broadcast_to(mean, (SEQ, LANES))
        stats[rows, LANES:] = jnp.broadcast_to(inv, (SEQ, LANES))

    project(ns, cs, qkv_w, out_w, qkv, og)
    attend(qkv, og, dqkv, att, 2)

    eight = eight_rows((main, width))
    nt1[...] = nt(eight, ns[...]).astype(BF16)
    at1[...] = nt(eight, att[...]).astype(BF16)
    targets = places(pairs, FIRST)
    for kind in range(2):
        for c in range(0, width, TILE):
            q, k, v = (slice(part * width + c, part * width + c + TILE) for part in range(3))
            if kind == 0:
                low, high = nn(nt1[...], dqkv[:, q]), nn(nt1[...], dqkv[:, k])
            else:
                low, high = nn(nt1[...], dqkv[:, v]), nn(at1[...], cs[:, q])
            share(bits, next(targets), low, high)


def places(pairs, streams):
    for i, stream in enumerate(streams):
        for c in range(0, stream[2] * TILE, TILE):
            yield stream, pairs[i], pairs[len(streams) + i], c


def share(bits, target, low, high):
    ((_, bit), *_), keep, send, c = target
    same = is_own(lax.broadcasted_iota(jnp.int32, low.shape, 0), bits, bit)
    keep[:, c : c + TILE] = jnp.where(same, low, high).astype(BF16)
    send[:, c : c + TILE] = jnp.where(same, high, low).astype(BF16)


def main_part(bits, got, qkv_weight, out_weight, tokens):
    width = out_weight.shape[0]
    main = got.shape[0]
    vmem = pl.BlockSpec(memory_space=pltpu.VMEM)
    square = (tokens, width)
    outs = [(square, BF16), (square, BF16), ((tokens, 2 * LANES), F32), ((tokens, 3 * width), BF16)]
    outs += [(square, BF16), (square, BF16)]
    outs += [((main, stream[2] * TILE), BF16) for stream in FIRST * 2]
    return pl.pallas_call(
        main_kernel,
        in_specs=[pl.BlockSpec(memory_space=pltpu.SMEM)] + [vmem] * 3,
        out_specs=[vmem] * len(outs),
        out_shape=[jax.ShapeDtypeStruct(s, d) for s, d in outs],
        scratch_shapes=[
            pltpu.VMEM((main, tokens), BF16),
            pltpu.VMEM((main, tokens), BF16),
            pltpu.VMEM((tokens, 3 * width), BF16),
            pltpu.VMEM(square, BF16),
            pltpu.VMEM((main, main), BF16),
        ],
        name="main_part",
        **parameters(34, 16 * 10**9, 30 * 10**6),
    )(bits, got, qkv_weight, out_weight)


def rest_kernel(bits, cs, dqkv, ns, att, *refs):
    *pairs, nt2, at2 = refs
    tokens, width = cs.shape
    main = 2 * nt2.shape[0]
    four = four_rows((main // 2, width))
    nt2[...] = nt(four, ns[...]).astype(BF16)
    at2[...] = nt(four, att[...]).astype(BF16)
    is_upper = lax.broadcasted_iota(jnp.int32, (main // 16, 8, TILE), 1) < 4

    def under(a, b):
        a, b = a.reshape(is_upper.shape), b.reshape(is_upper.shape)
        first = jnp.where(is_upper, a, pltpu.roll(b, 4, 1))
        second = jnp.where(is_upper, pltpu.roll(a, 4, 1), b)
        return jnp.stack([first, second], axis=1).reshape(main, TILE)

    targets = places(pairs, LAST)
    for c in range(0, width, TILE):
        q, k, v = (slice(part * width + c, part * width + c + TILE) for part in range(3))
        low = under(nn(nt2[...], dqkv[:, q]), nn(nt2[...], dqkv[:, v]))
        high = under(nn(nt2[...], dqkv[:, k]), nn(at2[...], cs[:, q]))
        share(bits, next(targets), low, high)


def rest_part(bits, cs, dqkv, ns, att, main):
    tokens = cs.shape[0]
    vmem = pl.BlockSpec(memory_space=pltpu.VMEM)
    shapes = [(main, stream[2] * TILE) for stream in LAST * 2]
    return pl.pallas_call(
        rest_kernel,
        in_specs=[pl.BlockSpec(memory_space=pltpu.SMEM)] + [vmem] * 4,
        out_specs=[vmem] * len(shapes),
        out_shape=[jax.ShapeDtypeStruct(s, BF16) for s in shapes],
        scratch_shapes=[pltpu.VMEM((main // 2, tokens), BF16)] * 2,
        name="rest_part",
        **parameters(24, 10**6, 10**5),
    )(bits, cs, dqkv, ns, att)


def token_kernel(xs, cs, stats, dqkv, qkv_w, out, ngs, igs):
    tokens, width = xs.shape
    main = out.shape[0]
    rest = tokens - main
    half = width // 2
    for f in range(0, width, 256):
        ngs[:, f : f + 256] = nt(dqkv[...], qkv_w[f : f + 256, :])

    @pl.loop(0, tokens // SEQ, unroll=12)
    def _(g):
        rows = rows_of(g)
        inv = stats[rows, LANES:][:, :1]
        xhat = (xs[rows, :].astype(F32) - stats[rows, :LANES][:, :1]) * inv
        ng = ngs[rows, :]
        centred = ng - jnp.mean(ng, axis=-1, keepdims=True)
        centred = centred - xhat * jnp.mean(ng * xhat, axis=-1, keepdims=True)
        igs[rows, :] = (cs[rows, :].astype(F32) + inv * centred).astype(BF16)

    back = one_hot((main, main), lambda i: (i % 8) * SEQ + i // 8)
    for c in range(0, width, half):
        out[:, c : c + half] = nn(back, igs[:main, c : c + half]).astype(BF16)
    tail = nn(back[:, :rest], igs[main:, :half]) + nn(back[:, rest:], igs[main:, half:])
    out[:, width:] = tail.astype(BF16)


def token_part(xs, cs, stats, dqkv, qkv_weight, main):
    tokens, width = xs.shape
    vmem = pl.BlockSpec(memory_space=pltpu.VMEM)
    return pl.pallas_call(
        token_kernel,
        in_specs=[vmem] * 5,
        out_specs=vmem,
        out_shape=jax.ShapeDtypeStruct((main, width + width // 2), BF16),
        scratch_shapes=[pltpu.VMEM((tokens, width), F32), pltpu.VMEM((tokens, width), BF16)],
        name="token_grad",
        **parameters(20, 10**6, 10**5),
    )(xs, cs, stats, dqkv, qkv_weight)


def join_kernel(streams, bits, *refs):
    count = len(streams)
    kept, came, kept_on, sent_on = (refs[i * count : (i + 1) * count] for i in range(4))
    half = TILE // 2
    for i, (_, (_, bit), blocks) in enumerate(streams):
        for c in range(blocks):
            at = c * TILE
            both = kept[i][:, at : at + TILE].astype(F32) + came[i][:, at : at + TILE].astype(F32)
            low, high = both[:, :half], both[:, half:]
            same = is_own(lax.broadcasted_iota(jnp.int32, low.shape, 0), bits, bit)
            kept_on[i][:, c * half : (c + 1) * half] = jnp.where(same, low, high).astype(BF16)
            sent_on[i][:, c * half : (c + 1) * half] = jnp.where(same, high, low).astype(BF16)


def join(streams, bits, pairs):
    vmem = pl.BlockSpec(memory_space=pltpu.VMEM)
    shapes = [(a.shape[0], a.shape[1] // 2) for a in pairs]
    return pl.pallas_call(
        functools.partial(join_kernel, streams),
        in_specs=[pl.BlockSpec(memory_space=pltpu.SMEM)] + [vmem] * len(pairs),
        out_specs=[vmem] * len(pairs),
        out_shape=[jax.ShapeDtypeStruct(s, BF16) for s in shapes],
        name="join",
        **parameters(16, 10**4, 10**4),
    )(bits, *pairs)


def join_last_kernel(grad, *refs):
    *pairs, out = refs
    at = grad.shape[1]
    out[:, :at] = grad[...]
    for keep, came in zip(pairs[: len(STREAMS)], pairs[len(STREAMS) :], strict=True):
        count = keep.shape[1]
        out[:, at : at + count] = (keep[...].astype(F32) + came[...].astype(F32)).astype(BF16)
        at += count


def join_last(grad, pairs):
    vmem = pl.BlockSpec(memory_space=pltpu.VMEM)
    width = grad.shape[1] + sum(a.shape[1] for a in pairs) // 2
    return pl.pallas_call(
        join_last_kernel,
        in_specs=[vmem] * (1 + len(pairs)),
        out_specs=vmem,
        out_shape=jax.ShapeDtypeStruct((grad.shape[0], width), BF16),
        name="join_last",
        **parameters(16, 0, 4 * 10**6),
    )(grad, *pairs)


def finish_kernel(bits, got, grad, qkv_grad, out_grad, total):
    rows, width = got.shape[0], out_grad.shape[1]
    packed = width + width // 2
    grad[:rows, :] = got[:, :width]
    part = 128
    pick = one_hot((part // 2, part), lambda k: (k // 4) * 8 + k % 4)
    pick_low = one_hot((part // 2, part), lambda k: (k // 4) * 8 + 4 + k % 4)
    for i in range(0, rows, part):
        tail = slice(rows + i // 2, rows + (i + part) // 2)
        grad[tail, : width // 2] = nn(pick, got[i : i + part, width:packed]).astype(BF16)
        grad[tail, width // 2 :] = nn(pick_low, got[i : i + part, width:packed]).astype(BF16)
    peers = got.shape[0] // 8
    half = TILE // 2
    blocks = width // TILE
    places = [stream for stream in STREAMS for _ in range(stream[2])]
    for block, ((_, first), (_, second), _) in enumerate(places):
        at = packed + block * half
        came = got[:, at : at + half].astype(F32)
        sums = {}
        for s in range(peers):
            key = (s >> first) & 1, (s >> second) & 1
            more = came[8 * s : 8 * s + 8]
            sums[key] = sums[key] + more if key in sums else more
        at = (2 * (block // blocks) * blocks + block % blocks) * TILE
        for i in range(2):
            for j in range(2):
                mine = [jnp.where(bits[second] == j, sums[a, 0], sums[a, 1]) for a in range(2)]
                to = at + i * width + j * half
                total[:, to : to + half] = jnp.where(bits[first] == i, mine[0], mine[1])
    q, k, v, o, low, high = (total[:, i * width : (i + 1) * width] for i in range(6))
    for part, (top, end) in enumerate(((q, low[:4]), (k, high[:4]), (v, low[4:]))):
        qkv_grad[:8, part * width : (part + 1) * width] = top
        qkv_grad[8:12, part * width : (part + 1) * width] = end
    out_grad[:8, :] = o
    out_grad[8:12, :] = high[4:]


def finish(bits, got, tokens, width):
    vmem = pl.BlockSpec(memory_space=pltpu.VMEM)
    return pl.pallas_call(
        finish_kernel,
        in_specs=[pl.BlockSpec(memory_space=pltpu.SMEM), vmem],
        out_specs=[vmem] * 3,
        out_shape=[jax.ShapeDtypeStruct((tokens, width), BF16)]
        + [jax.ShapeDtypeStruct((12, n), F32) for n in (3 * width, width)],
        scratch_shapes=[pltpu.VMEM((8, 6 * width), F32)],
        name="finish",
        **parameters(16, 10**7, 2 * 10**6),
    )(bits, got)


def local(activations, cotangent, qkv_weight, out_weight):
    grid_rows, grid_cols = lax.axis_size("row"), lax.axis_size("col")
    peers = grid_rows * grid_cols
    rows_dev, cols_dev, width = activations.shape
    tokens = rows_dev * cols_dev
    exchange = functools.partial(
        lax.all_to_all, axis_name=("row", "col"), split_axis=0, concat_axis=0, tiled=True
    )
    row, col = lax.axis_index("row"), lax.axis_index("col")
    place = row * grid_cols + col
    bits = jnp.stack([place // (1 << bit) % 2 for bit in range(6)]).astype(jnp.int32)
    sent = pack_tokens(activations.reshape(tokens, width), cotangent.reshape(tokens, width), peers)
    sent, bits = lax.optimization_barrier((sent, bits))
    xs, cs, stats, dqkv, ns, att, *early = main_part(bits, exchange(sent), qkv_weight, out_weight, tokens)

    def swap(arrays, streams, level):
        return [
            lax.ppermute(x, ("row", "col"), [(i, i ^ stream[level][0]) for i in range(peers)])
            for x, stream in zip(arrays, streams, strict=True)
        ]

    first, last = len(FIRST), len(LAST)
    early_came = swap(early[first:], FIRST, 0)
    late = rest_part(bits, cs, dqkv, ns, att, peers * 8)
    late_came = swap(late[last:], LAST, 0)
    dqkv, *_ = lax.optimization_barrier((dqkv, *late))
    grads = token_part(xs, cs, stats, dqkv, qkv_weight, peers * 8)
    grads, *early_came = lax.optimization_barrier((grads, *early_came))
    early = join(FIRST, bits, (*early[:first], *early_came))
    early_came = swap(early[first:], FIRST, 1)
    grads, *late_came = lax.optimization_barrier((grads, *late_came))
    late = join(LAST, bits, (*late[:last], *late_came))
    late_came = swap(late[last:], LAST, 1)
    got = exchange(join_last(grads, (*early[:first], *late[:last], *early_came, *late_came)))
    input_grad, qkv_weight_grad, out_weight_grad = finish(bits, got, tokens, width)
    return (input_grad.reshape(rows_dev, cols_dev, width), qkv_weight_grad, out_weight_grad)


def solution(mesh):
    return jax.shard_map(
        local,
        mesh=mesh,
        in_specs=(P(("scene", "row"), "col", None), P(("scene", "row"), "col", None), P(), P()),
        out_specs=(
            P(("scene", "row"), "col", None),
            P(("scene", "row", "col"), None),
            P(("scene", "row", "col"), None),
        ),
        check_vma=False,
    )
```

```python
import functools

import jax
import jax.numpy as jnp
from jax import lax
from jax.experimental import pallas as pl
from jax.experimental.pallas import tpu as pltpu
from jax.sharding import PartitionSpec as P

HEADS = 24
EPSILON = 1e-05
BF16 = jnp.bfloat16
F32 = jnp.float32
MIB = 1 << 20


SEQ = 64
LANES = 128
LOG2_E = 1.4426950408889634
FIRST = (((16, 4), (8, 3), 2), ((48, 5), (2, 1), 2), ((8, 3), (16, 4), 2))
LAST = (((2, 1), (48, 5), 1), ((6, 2), (9, 0), 1), ((9, 0), (6, 2), 1))
STREAMS = FIRST + LAST
TILE = 256


def dot(a, b, dims):
    return lax.dot_general(a, b, ((dims[0], dims[1]), ((), ())), preferred_element_type=F32)


def nn(a, b):
    return dot(a, b, ((1,), (0,)))


def nt(a, b):
    return dot(a, b, ((1,), (1,)))


def tn(a, b):
    return dot(a, b, ((0,), (0,)))


def one_hot(shape, column_of_row):
    rows = lax.broadcasted_iota(jnp.int32, shape, 0)
    columns = lax.broadcasted_iota(jnp.int32, shape, 1)
    return jnp.where(columns == column_of_row(rows), 1.0, 0.0).astype(BF16)


def pack_kernel(act_main, act_tail, cot_main, cot_tail, out):
    rows, width = act_main.shape
    half = width // 2
    upper = one_hot((rows, rows // 2), lambda i: jnp.where(i % 8 < 4, (i // 8) * 4 + i % 4, -1))
    lower = one_hot((rows, rows // 2), lambda i: jnp.where(i % 8 < 4, -1, (i // 8) * 4 + i % 4))
    at = 0
    for main, tail in ((act_main, act_tail), (cot_main, cot_tail)):
        out[:, at : at + width] = main[...]
        packed = nn(upper, tail[:, :half]) + nn(lower, tail[:, half:])
        out[:, at + width : at + width + half] = packed.astype(BF16)
        at += width + half


def pack_tokens(act, cot, peers):
    tokens, width = act.shape
    steps = 4
    rows = peers * 8 // steps
    main = pl.BlockSpec((rows, width), lambda i: (i, 0))
    tail = pl.BlockSpec((rows // 2, width), lambda i: (2 * steps + i, 0))
    return pl.pallas_call(
        pack_kernel,
        grid=(steps,),
        in_specs=[main, tail, main, tail],
        out_specs=pl.BlockSpec((rows, 3 * width), lambda i: (i, 0)),
        out_shape=jax.ShapeDtypeStruct((peers * 8, 3 * width), BF16),
        compiler_params=pltpu.CompilerParams(vmem_limit_bytes=32 * MIB),
        name="pack_tokens",
    )(act, act, cot, cot)


def parameters(limit, flops=0, moved=0):
    return dict(
        compiler_params=pltpu.CompilerParams(vmem_limit_bytes=limit * MIB),
        cost_estimate=pl.CostEstimate(flops=flops, bytes_accessed=moved, transcendentals=0),
    )


def is_own(row, bits, bit):
    return (row // (8 << bit)) % 2 == bits[bit]


def rows_of(g):
    return pl.ds(pl.multiple_of(g * SEQ, SEQ), SEQ)


def project(ns, cs, qkv_w, out_w, qkv, og):
    for c in range(0, qkv.shape[1], 256):
        qkv[:, c : c + 256] = nn(ns[...], qkv_w[:, c : c + 256]).astype(BF16)
    for c in range(0, og.shape[1], 256):
        og[:, c : c + 256] = nt(cs[...], out_w[c : c + 256, :]).astype(BF16)


def attend(qkv, og, dqkv, att, together):
    tokens, count = og.shape
    head_dim = 32
    scaling = head_dim**-0.5
    heads = LANES // head_dim
    shape = (heads * SEQ, LANES)
    own = lax.broadcasted_iota(jnp.int32, shape, 0) // SEQ
    keep = jnp.where(lax.broadcasted_iota(jnp.int32, shape, 1) // head_dim == own, 1.0, 0.0).astype(BF16)
    lane_head = lax.broadcasted_iota(jnp.int32, (SEQ, LANES), 1) // head_dim

    def spread(x):
        return jnp.concatenate([x] * heads, axis=0) * keep

    def fold(x):
        total = x[:SEQ]
        for h in range(1, heads):
            total = jnp.where(lane_head == h, x[h * SEQ : (h + 1) * SEQ], total)
        return total

    @pl.loop(0, tokens // SEQ // together)
    def _(step):
        blocks = [(rows_of(step * together + g), c) for g in range(together) for c in range(0, count, LANES)]
        queries = [qkv[rows, c : c + LANES] for rows, c in blocks]
        keys = [qkv[rows, count + c : count + c + LANES] for rows, c in blocks]
        values = [qkv[rows, 2 * count + c : 2 * count + c + LANES] for rows, c in blocks]
        q_wide = [spread(q) for q in queries]
        g_wide = [spread(og[rows, c : c + LANES]) for rows, c in blocks]
        scores = [nt(k, q) for k, q in zip(keys, q_wide)]
        prob_grads = [nt(v, g) for v, g in zip(values, g_wide)]
        probs_low, score_low = [], []
        for score, prob_grad in zip(scores, prob_grads):
            top = jnp.max(score, axis=0, keepdims=True)
            e = jnp.exp2((score - top) * (scaling * LOG2_E))
            probs = e * (1.0 / jnp.sum(e, axis=0, keepdims=True))
            delta = jnp.sum(probs * prob_grad, axis=0, keepdims=True)
            probs_low.append(probs.astype(BF16))
            score_low.append((probs * (prob_grad - delta)).astype(BF16))
        value_grads = [nn(p, g) for p, g in zip(probs_low, g_wide)]
        key_grads = [nn(s, q) for s, q in zip(score_low, q_wide)]
        attended = [tn(p, v) for p, v in zip(probs_low, values)]
        query_grads = [tn(s, k) for s, k in zip(score_low, keys)]
        for i, (rows, c) in enumerate(blocks):
            dqkv[rows, count + c : count + c + LANES] = (key_grads[i] * scaling).astype(BF16)
            dqkv[rows, 2 * count + c : 2 * count + c + LANES] = value_grads[i].astype(BF16)
            att[rows, c : c + LANES] = fold(attended[i]).astype(BF16)
            dqkv[rows, c : c + LANES] = (fold(query_grads[i]) * scaling).astype(BF16)


def eight_rows(shape):
    return one_hot(shape, lambda i: (i // 8) * 12 + i % 8)


def four_rows(shape):
    return one_hot(shape, lambda i: (i // 4) * 12 + 8 + i % 4)


def main_kernel(
    bits, got, qkv_w, out_w, xs, cs, stats, dqkv, *refs
):
    ns, att, *pairs = refs[: 2 + 2 * len(FIRST)]
    nt1, at1, qkv, og, order = refs[2 + 2 * len(FIRST) :]
    width = out_w.shape[0]
    half = width // 2
    tokens = xs.shape[0]
    main = got.shape[0]
    rest = tokens - main
    packed = width + half

    order[...] = one_hot((main, main), lambda k: (k % SEQ) * 8 + k // SEQ)
    for first, to in ((0, xs), (packed, cs)):
        for c in range(0, width, half):
            to[:main, c : c + half] = nn(order[...], got[:, first + c : first + c + half]).astype(BF16)
        tail = nn(order[...], got[:, first + width : first + packed]).astype(BF16)
        to[main:, :half] = tail[:rest]
        to[main:, half:] = tail[rest:]

    @pl.loop(0, tokens // SEQ, unroll=12)
    def _(g):
        rows = rows_of(g)
        x = xs[rows, :].astype(F32)
        mean = jnp.mean(x, axis=-1, keepdims=True)
        centred = x - mean
        inv = lax.rsqrt(jnp.mean(centred * centred, axis=-1, keepdims=True) + EPSILON)
        ns[rows, :] = (centred * inv).astype(BF16)
        stats[rows, :LANES] = jnp.broadcast_to(mean, (SEQ, LANES))
        stats[rows, LANES:] = jnp.broadcast_to(inv, (SEQ, LANES))

    project(ns, cs, qkv_w, out_w, qkv, og)
    attend(qkv, og, dqkv, att, 2)

    eight = eight_rows((main, width))
    nt1[...] = nt(eight, ns[...]).astype(BF16)
    at1[...] = nt(eight, att[...]).astype(BF16)
    targets = places(pairs, FIRST)
    for kind in range(2):
        for c in range(0, width, TILE):
            q, k, v = (slice(part * width + c, part * width + c + TILE) for part in range(3))
            if kind == 0:
                low, high = nn(nt1[...], dqkv[:, q]), nn(nt1[...], dqkv[:, k])
            else:
                low, high = nn(nt1[...], dqkv[:, v]), nn(at1[...], cs[:, q])
            share(bits, next(targets), low, high)


def places(pairs, streams):
    for i, stream in enumerate(streams):
        for c in range(0, stream[2] * TILE, TILE):
            yield stream, pairs[i], pairs[len(streams) + i], c


def share(bits, target, low, high):
    ((_, bit), *_), keep, send, c = target
    same = is_own(lax.broadcasted_iota(jnp.int32, low.shape, 0), bits, bit)
    keep[:, c : c + TILE] = jnp.where(same, low, high).astype(BF16)
    send[:, c : c + TILE] = jnp.where(same, high, low).astype(BF16)


def main_part(bits, got, qkv_weight, out_weight, tokens):
    width = out_weight.shape[0]
    main = got.shape[0]
    vmem = pl.BlockSpec(memory_space=pltpu.VMEM)
    square = (tokens, width)
    outs = [(square, BF16), (square, BF16), ((tokens, 2 * LANES), F32), ((tokens, 3 * width), BF16)]
    outs += [(square, BF16), (square, BF16)]
    outs += [((main, stream[2] * TILE), BF16) for stream in FIRST * 2]
    return pl.pallas_call(
        main_kernel,
        in_specs=[pl.BlockSpec(memory_space=pltpu.SMEM)] + [vmem] * 3,
        out_specs=[vmem] * len(outs),
        out_shape=[jax.ShapeDtypeStruct(s, d) for s, d in outs],
        scratch_shapes=[
            pltpu.VMEM((main, tokens), BF16),
            pltpu.VMEM((main, tokens), BF16),
            pltpu.VMEM((tokens, 3 * width), BF16),
            pltpu.VMEM(square, BF16),
            pltpu.VMEM((main, main), BF16),
        ],
        name="main_part",
        **parameters(34, 16 * 10**9, 30 * 10**6),
    )(bits, got, qkv_weight, out_weight)


def rest_kernel(bits, cs, dqkv, ns, att, *refs):
    *pairs, nt2, at2 = refs
    tokens, width = cs.shape
    main = 2 * nt2.shape[0]
    four = four_rows((main // 2, width))
    nt2[...] = nt(four, ns[...]).astype(BF16)
    at2[...] = nt(four, att[...]).astype(BF16)
    is_upper = lax.broadcasted_iota(jnp.int32, (main // 16, 8, TILE), 1) < 4

    def under(a, b):
        a, b = a.reshape(is_upper.shape), b.reshape(is_upper.shape)
        first = jnp.where(is_upper, a, pltpu.roll(b, 4, 1))
        second = jnp.where(is_upper, pltpu.roll(a, 4, 1), b)
        return jnp.stack([first, second], axis=1).reshape(main, TILE)

    targets = places(pairs, LAST)
    for c in range(0, width, TILE):
        q, k, v = (slice(part * width + c, part * width + c + TILE) for part in range(3))
        low = under(nn(nt2[...], dqkv[:, q]), nn(nt2[...], dqkv[:, v]))
        high = under(nn(nt2[...], dqkv[:, k]), nn(at2[...], cs[:, q]))
        share(bits, next(targets), low, high)


def rest_part(bits, cs, dqkv, ns, att, main):
    tokens = cs.shape[0]
    vmem = pl.BlockSpec(memory_space=pltpu.VMEM)
    shapes = [(main, stream[2] * TILE) for stream in LAST * 2]
    return pl.pallas_call(
        rest_kernel,
        in_specs=[pl.BlockSpec(memory_space=pltpu.SMEM)] + [vmem] * 4,
        out_specs=[vmem] * len(shapes),
        out_shape=[jax.ShapeDtypeStruct(s, BF16) for s in shapes],
        scratch_shapes=[pltpu.VMEM((main // 2, tokens), BF16)] * 2,
        name="rest_part",
        **parameters(24, 10**6, 10**5),
    )(bits, cs, dqkv, ns, att)


def token_kernel(xs, cs, stats, dqkv, qkv_w, out, ngs, igs):
    tokens, width = xs.shape
    main = out.shape[0]
    rest = tokens - main
    half = width // 2
    for f in range(0, width, 256):
        ngs[:, f : f + 256] = nt(dqkv[...], qkv_w[f : f + 256, :])

    @pl.loop(0, tokens // SEQ, unroll=12)
    def _(g):
        rows = rows_of(g)
        inv = stats[rows, LANES:][:, :1]
        xhat = (xs[rows, :].astype(F32) - stats[rows, :LANES][:, :1]) * inv
        ng = ngs[rows, :]
        centred = ng - jnp.mean(ng, axis=-1, keepdims=True)
        centred = centred - xhat * jnp.mean(ng * xhat, axis=-1, keepdims=True)
        igs[rows, :] = (cs[rows, :].astype(F32) + inv * centred).astype(BF16)

    back = one_hot((main, main), lambda i: (i % 8) * SEQ + i // 8)
    for c in range(0, width, half):
        out[:, c : c + half] = nn(back, igs[:main, c : c + half]).astype(BF16)
    tail = nn(back[:, :rest], igs[main:, :half]) + nn(back[:, rest:], igs[main:, half:])
    out[:, width:] = tail.astype(BF16)


def token_part(xs, cs, stats, dqkv, qkv_weight, main):
    tokens, width = xs.shape
    vmem = pl.BlockSpec(memory_space=pltpu.VMEM)
    return pl.pallas_call(
        token_kernel,
        in_specs=[vmem] * 5,
        out_specs=vmem,
        out_shape=jax.ShapeDtypeStruct((main, width + width // 2), BF16),
        scratch_shapes=[pltpu.VMEM((tokens, width), F32), pltpu.VMEM((tokens, width), BF16)],
        name="token_grad",
        **parameters(20, 10**6, 10**5),
    )(xs, cs, stats, dqkv, qkv_weight)


def join_kernel(streams, bits, *refs):
    count = len(streams)
    kept, came, kept_on, sent_on = (refs[i * count : (i + 1) * count] for i in range(4))
    half = TILE // 2
    for i, (_, (_, bit), blocks) in enumerate(streams):
        for c in range(blocks):
            at = c * TILE
            both = kept[i][:, at : at + TILE].astype(F32) + came[i][:, at : at + TILE].astype(F32)
            low, high = both[:, :half], both[:, half:]
            same = is_own(lax.broadcasted_iota(jnp.int32, low.shape, 0), bits, bit)
            kept_on[i][:, c * half : (c + 1) * half] = jnp.where(same, low, high).astype(BF16)
            sent_on[i][:, c * half : (c + 1) * half] = jnp.where(same, high, low).astype(BF16)


def join(streams, bits, pairs):
    vmem = pl.BlockSpec(memory_space=pltpu.VMEM)
    shapes = [(a.shape[0], a.shape[1] // 2) for a in pairs]
    return pl.pallas_call(
        functools.partial(join_kernel, streams),
        in_specs=[pl.BlockSpec(memory_space=pltpu.SMEM)] + [vmem] * len(pairs),
        out_specs=[vmem] * len(pairs),
        out_shape=[jax.ShapeDtypeStruct(s, BF16) for s in shapes],
        name="join",
        **parameters(16, 10**4, 10**4),
    )(bits, *pairs)


def join_last_kernel(grad, *refs):
    *pairs, out = refs
    at = grad.shape[1]
    out[:, :at] = grad[...]
    for keep, came in zip(pairs[: len(STREAMS)], pairs[len(STREAMS) :], strict=True):
        count = keep.shape[1]
        out[:, at : at + count] = (keep[...].astype(F32) + came[...].astype(F32)).astype(BF16)
        at += count


def join_last(grad, pairs):
    vmem = pl.BlockSpec(memory_space=pltpu.VMEM)
    width = grad.shape[1] + sum(a.shape[1] for a in pairs) // 2
    return pl.pallas_call(
        join_last_kernel,
        in_specs=[vmem] * (1 + len(pairs)),
        out_specs=vmem,
        out_shape=jax.ShapeDtypeStruct((grad.shape[0], width), BF16),
        name="join_last",
        **parameters(16, 0, 4 * 10**6),
    )(grad, *pairs)


def finish_kernel(bits, got, grad, qkv_grad, out_grad, total):
    rows, width = got.shape[0], out_grad.shape[1]
    packed = width + width // 2
    grad[:rows, :] = got[:, :width]
    part = 128
    pick = one_hot((part // 2, part), lambda k: (k // 4) * 8 + k % 4)
    pick_low = one_hot((part // 2, part), lambda k: (k // 4) * 8 + 4 + k % 4)
    for i in range(0, rows, part):
        tail = slice(rows + i // 2, rows + (i + part) // 2)
        grad[tail, : width // 2] = nn(pick, got[i : i + part, width:packed]).astype(BF16)
        grad[tail, width // 2 :] = nn(pick_low, got[i : i + part, width:packed]).astype(BF16)
    peers = got.shape[0] // 8
    half = TILE // 2
    blocks = width // TILE
    places = [stream for stream in STREAMS for _ in range(stream[2])]
    for block, ((_, first), (_, second), _) in enumerate(places):
        at = packed + block * half
        came = got[:, at : at + half].astype(F32)
        sums = {}
        for s in range(peers):
            key = (s >> first) & 1, (s >> second) & 1
            more = came[8 * s : 8 * s + 8]
            sums[key] = sums[key] + more if key in sums else more
        at = (2 * (block // blocks) * blocks + block % blocks) * TILE
        for i in range(2):
            for j in range(2):
                mine = [jnp.where(bits[second] == j, sums[a, 0], sums[a, 1]) for a in range(2)]
                to = at + i * width + j * half
                total[:, to : to + half] = jnp.where(bits[first] == i, mine[0], mine[1])
    q, k, v, o, low, high = (total[:, i * width : (i + 1) * width] for i in range(6))
    for part, (top, end) in enumerate(((q, low[:4]), (k, high[:4]), (v, low[4:]))):
        qkv_grad[:8, part * width : (part + 1) * width] = top
        qkv_grad[8:12, part * width : (part + 1) * width] = end
    out_grad[:8, :] = o
    out_grad[8:12, :] = high[4:]


def finish(bits, got, tokens, width):
    vmem = pl.BlockSpec(memory_space=pltpu.VMEM)
    return pl.pallas_call(
        finish_kernel,
        in_specs=[pl.BlockSpec(memory_space=pltpu.SMEM), vmem],
        out_specs=[vmem] * 3,
        out_shape=[jax.ShapeDtypeStruct((tokens, width), BF16)]
        + [jax.ShapeDtypeStruct((12, n), F32) for n in (3 * width, width)],
        scratch_shapes=[pltpu.VMEM((8, 6 * width), F32)],
        name="finish",
        **parameters(16, 10**7, 2 * 10**6),
    )(bits, got)


def local(activations, cotangent, qkv_weight, out_weight):
    grid_rows, grid_cols = lax.axis_size("row"), lax.axis_size("col")
    peers = grid_rows * grid_cols
    rows_dev, cols_dev, width = activations.shape
    tokens = rows_dev * cols_dev
    exchange = functools.partial(
        lax.all_to_all, axis_name=("row", "col"), split_axis=0, concat_axis=0, tiled=True
    )
    row, col = lax.axis_index("row"), lax.axis_index("col")
    place = row * grid_cols + col
    bits = jnp.stack([place // (1 << bit) % 2 for bit in range(6)]).astype(jnp.int32)
    sent = pack_tokens(activations.reshape(tokens, width), cotangent.reshape(tokens, width), peers)
    sent, bits = lax.optimization_barrier((sent, bits))
    xs, cs, stats, dqkv, ns, att, *early = main_part(bits, exchange(sent), qkv_weight, out_weight, tokens)

    def swap(arrays, streams, level):
        return [
            lax.ppermute(x, ("row", "col"), [(i, i ^ stream[level][0]) for i in range(peers)])
            for x, stream in zip(arrays, streams, strict=True)
        ]

    first, last = len(FIRST), len(LAST)
    early_came = swap(early[first:], FIRST, 0)
    late = rest_part(bits, cs, dqkv, ns, att, peers * 8)
    late_came = swap(late[last:], LAST, 0)
    dqkv, *_ = lax.optimization_barrier((dqkv, *late))
    grads = token_part(xs, cs, stats, dqkv, qkv_weight, peers * 8)
    grads, *early_came = lax.optimization_barrier((grads, *early_came))
    early = join(FIRST, bits, (*early[:first], *early_came))
    early_came = swap(early[first:], FIRST, 1)
    grads, *late_came = lax.optimization_barrier((grads, *late_came))
    late = join(LAST, bits, (*late[:last], *late_came))
    late_came = swap(late[last:], LAST, 1)
    got = exchange(join_last(grads, (*early[:first], *late[:last], *early_came, *late_came)))
    input_grad, qkv_weight_grad, out_weight_grad = finish(bits, got, tokens, width)
    return (input_grad.reshape(rows_dev, cols_dev, width), qkv_weight_grad, out_weight_grad)


def solution(mesh):
    return jax.shard_map(
        local,
        mesh=mesh,
        in_specs=(P(("scene", "row"), "col", None), P(("scene", "row"), "col", None), P(), P()),
        out_specs=(
            P(("scene", "row"), "col", None),
            P(("scene", "row", "col"), None),
            P(("scene", "row", "col"), None),
        ),
        check_vma=False,
    )
```
